32 devices in a mesh: band: 4 (over x, core), blk: 8 (over z, y).
Axes of the slice: x: 2, y: 2, z: 4, core: 2. Of those that a mesh axis runs over, the one named last changes fastest.
Arguments:
- visibility: float32 [2, 32, 8192], P(None, 'band', 'blk'), may hold values from -6 to 6
- coherency: float32 [2, 32, 100, 8192], P(None, 'band', None, 'blk'), may hold values from -0.625 to 0.625
- station_first: int32 [8192], P('blk'), may hold values from 0 to 61, as said below
- station_second: int32 [8192], P('blk'), may hold values from 0 to 61
- gains_start: float32 [2, 62, 3200], P(None, None, 'band'), may hold values from -6 to 6
- consensus_prev: float32 [2, 62, 3200], P(None, None, 'band'), may hold values from -6 to 6
- dual_prev: float32 [2, 62, 3200], P(None, None, 'band'), may hold values from -6 to 6
- penalty: float32 [100], replicated, may hold values from 0.5 to 8
- noise_var: float32 [100], replicated, may hold values from 0.05 to 1
Outputs:
- gains: float32 [2, 62, 3200], P(None, None, 'band')
- consensus: float32 [2, 62, 3200], P(None, None, 'band')
- dual: float32 [2, 62, 3200], P(None, None, 'band')
The draws below stay inside these ranges and needn't reach their ends.
Inputs may be any that keep to these rules, and one draw needn't show every extreme that they name: station_first and station_second differ in every row.
All inputs are finite; a program needn't handle non-finite values.
Results may differ from the reference program's by a relative error of at most 0.0003.
Values sent between devices are 32-bit elements; how exact they have to be, the bound alone decides.
A program may use at most 128 MiB of HBM per device.

```python
import math
import jax
import jax.numpy as jnp
from jax import lax

P_SIZE = 62
K = 100
ITERS = 4
SB = 32
ROWS = 8192


def station_pairs(key):
    base = jax.random.fold_in(key, 7)
    first_key, step_key = jax.random.split(base)
    first = jax.random.randint(first_key, (ROWS,), 0, P_SIZE, dtype=jnp.int32)
    offset = jax.random.randint(step_key, (ROWS,), 1, P_SIZE, dtype=jnp.int32)
    second = (first + offset) % P_SIZE
    return (first, second)


def draw_station_first(key, part):
    return station_pairs(key)[0]


def draw_station_second(key, part):
    return station_pairs(key)[1]


def block_levels(rng, shape, pieces, least, top_value):
    factor_of, own = 1.0, jax.random.fold_in(rng, 6)
    for position, shards_of in pieces:
        draws = jnp.exp(jax.random.uniform(jax.random.fold_in(own, position), (shards_of,), jnp.float32, least / len(pieces), top_value / len(pieces)))
        factor_of = factor_of * jnp.repeat(draws, shape[position] // shards_of).reshape([-1 if axis == position else 1 for axis in range(len(shape))])
    return factor_of


def normal_values(key, shape, width, reach, cuts=(), kind=jnp.bfloat16):
    entries = jax.random.normal(key, shape, jnp.float32) * width
    if len(cuts) > 0:
        entries = block_levels(key, shape, cuts, -0.22, 0.18) * entries
    return jnp.clip(entries, min=-reach, max=reach).astype(kind)


def setup_inputs(seed: int = 0) -> dict:
    splits = jax.random.split(jax.random.key(seed), 10)
    return {
        "visibility": normal_values(splits[0], (2, SB, ROWS), 1.0, 6.0, ((1, 4), (2, 8)), jnp.float32),
        "coherency": normal_values(splits[1], (2, SB, K, ROWS), K ** -0.5, 0.625, ((1, 4), (3, 8)), jnp.float32),
        "station_first": draw_station_first(jax.random.fold_in(splits[9], 71), 0),
        "station_second": draw_station_second(jax.random.fold_in(splits[9], 71), 0),
        "gains_start": normal_values(splits[4], (2, P_SIZE, SB * K), 1.0, 6.0, ((2, 4),), jnp.float32),
        "consensus_prev": normal_values(splits[5], (2, P_SIZE, SB * K), 1.0, 6.0, ((2, 4),), jnp.float32),
        "dual_prev": normal_values(splits[6], (2, P_SIZE, SB * K), 1.0, 6.0, ((2, 4),), jnp.float32),
        "penalty": jnp.clip(jnp.exp(jax.random.uniform(splits[7], (K,), jnp.float32, math.log(0.5), math.log(8.0))), 0.5, 8.0),
        "noise_var": jnp.clip(jnp.exp(jax.random.uniform(splits[8], (K,), jnp.float32, math.log(0.05), math.log(1.0))), 0.05, 1.0),
    }


def band_sums(coh, vis, gains, first, second):
    gp_re = gains[0][first].T
    gp_im = gains[1][first].T
    gq_re = gains[0][second].T
    gq_im = gains[1][second].T
    c_re = coh[0]
    c_im = coh[1]
    t_re = c_re * gq_re + c_im * gq_im
    t_im = c_im * gq_re - c_re * gq_im
    m_re = gp_re * t_re - gp_im * t_im
    m_im = gp_re * t_im + gp_im * t_re
    e_re = vis[0] - jnp.sum(m_re, axis=0)
    e_im = vis[1] - jnp.sum(m_im, axis=0)
    r_re = e_re[None, :] + m_re
    r_im = e_im[None, :] + m_im
    u_re = c_re * gp_re - c_im * gp_im
    u_im = c_re * gp_im + c_im * gp_re

    def spread(x, index):
        return jax.ops.segment_sum(x.T, index, num_segments=P_SIZE)
    num_re = spread(r_re * t_re + r_im * t_im, first) + spread(r_re * u_re + r_im * u_im, second)
    num_im = spread(r_im * t_re - r_re * t_im, first) + spread(r_re * u_im - r_im * u_re, second)
    den = spread(t_re * t_re + t_im * t_im, first) + spread(u_re * u_re + u_im * u_im, second)
    return jnp.stack([num_re, num_im, den])

def smoother(noise, count):
    index = jnp.arange(count, dtype=jnp.float32)
    diff = (index[:, None] - index[None, :]) / (count / 4.0)
    kern = jnp.exp(-0.5 * diff * diff)

    def single(level):
        matrix = kern + level * jnp.eye(count, dtype=jnp.float32)
        factor = jnp.linalg.cholesky(matrix)
        return jax.scipy.linalg.cho_solve((factor, True), kern).T
    return jax.vmap(single)(noise)

def reference(visibility, coherency, station_first, station_second, gains_start, consensus_prev, dual_prev, penalty, noise_var):
    rho_col = jnp.tile(penalty, SB)
    weight = rho_col * (ROWS / (P_SIZE * K))
    target = consensus_prev - dual_prev / rho_col
    gains = gains_start
    for step in range(ITERS):
        view = gains.reshape(2, P_SIZE, SB, K)

        def one_band(index):
            coh = lax.dynamic_index_in_dim(coherency, index, 1, False)
            vis = lax.dynamic_index_in_dim(visibility, index, 1, False)
            gband = lax.dynamic_index_in_dim(view, index, 2, False)
            return band_sums(coh, vis, gband, station_first, station_second)
        parts = lax.map(one_band, jnp.arange(SB, dtype=jnp.int32))
        total = parts.transpose(1, 2, 0, 3).reshape(3, P_SIZE, SB * K)
        fresh_re = (total[0] + weight * target[0]) / (total[2] + weight)
        fresh_im = (total[1] + weight * target[1]) / (total[2] + weight)
        gains = 0.5 * gains + 0.5 * jnp.stack([fresh_re, fresh_im])
    mixed = (gains + dual_prev / rho_col).reshape(2, P_SIZE, SB, K)
    smooth = smoother(noise_var, SB)
    consensus = jnp.einsum('kfg,cpgk->cpfk', smooth, mixed, precision=lax.Precision.HIGHEST).reshape(2, P_SIZE, SB * K)
    dual = dual_prev + rho_col * (gains - consensus)
    return (gains, consensus, dual)
```

```python
import functools
import jax
import jax.numpy as jnp
from jax import lax
from jax.experimental import pallas as pl
from jax.experimental.pallas import tpu as pltpu
from jax.sharding import PartitionSpec as P

ITERS = 4
LANES = 128
HALF = 64
CHUNK = 256
TILE = 16


def round_up(x, m):
    return (x + m - 1) // m * m


def smoother_kernel(count, noise_ref, out_ref, work):
    level = noise_ref[...]
    cols = lax.broadcasted_iota(jnp.int32, (count, LANES), 0)
    for i in range(count):
        diff = (cols - i).astype(jnp.float32) / (count / 4.0)
        kern = jnp.exp(-0.5 * diff * diff)
        work[i, :count, :] = kern + jnp.where(cols == i, level, 0.0)
        work[i, count:, :] = kern

    def eliminate(p, carry):
        pivot = work[p, pl.ds(p, 1), :]
        row = work[p] / pivot
        for i in range(count):
            work[i] = work[i] - work[i, pl.ds(p, 1), :] * row
        work[p] = row
        return carry

    lax.fori_loop(0, count, eliminate, 0)
    for i in range(count):
        out_ref[i] = work[i, count:, :]


def smoother(noise, count):
    pad = jnp.pad(noise, (0, LANES * ((noise.shape[0] + LANES - 1) // LANES) - noise.shape[0]), constant_values=1.0)
    groups = pad.shape[0] // LANES
    return pl.pallas_call(
        functools.partial(smoother_kernel, count),
        out_shape=jax.ShapeDtypeStruct((count, count, groups * LANES), jnp.float32),
        grid=(groups,),
        in_specs=[pl.BlockSpec((1, LANES), lambda g: (0, g))],
        out_specs=pl.BlockSpec((count, count, LANES), lambda g: (0, 0, g)),
        scratch_shapes=[pltpu.VMEM((count, 2 * count, LANES), jnp.float32)],
        compiler_params=pltpu.CompilerParams(vmem_limit_bytes=16 << 20),
        name="smoother",
    )(pad[None, :])


def band_sums(g_re, g_im, load_c, load_v, rows, t1, t2, tt, gp, gq, xs):
    half_k = g_re.shape[0]
    full_k = 2 * half_k
    lane = lax.broadcasted_iota(jnp.int32, (half_k, LANES), 1)
    low = lane < HALF
    parts = []
    for g in (g_re, g_im):
        r = pltpu.roll(g, HALF, 1)
        for full in (jnp.where(low, g, r), jnp.where(low, r, g)):
            hi = full.astype(jnp.bfloat16).astype(jnp.float32)
            parts.append(jnp.where(low, hi, full - hi))
    lhs = jnp.concatenate(parts, axis=0).astype(jnp.bfloat16)
    total = None
    for rc in range(rows // CHUNK):
        buf = rc % 2
        rsl = pl.ds(rc * CHUNK, CHUNK)
        gp[buf] = jnp.dot(lhs, t1[:, rsl], preferred_element_type=jnp.float32)
        gq[buf] = jnp.dot(lhs, t2[:, rsl], preferred_element_type=jnp.float32)
        sum_re = jnp.zeros((TILE, CHUNK), jnp.float32)
        sum_im = jnp.zeros((TILE, CHUNK), jnp.float32)

        def put(kind, kt, side, x):
            hi = x.astype(jnp.bfloat16)
            lo = (x - hi.astype(jnp.float32)).astype(jnp.bfloat16)
            rsel = pl.ds(kind * full_k + kt * TILE, TILE)
            xs[buf, rsel, pl.ds(2 * side * CHUNK, CHUNK)] = hi
            xs[buf, rsel, pl.ds((2 * side + 1) * CHUNK, CHUNK)] = lo

        for kt in range(full_k // TILE):
            c_re, c_im = load_c(kt, rsl)
            sl_re, sl_im = pl.ds(kt * TILE, TILE), pl.ds(full_k + kt * TILE, TILE)
            p_re, p_im, q_re, q_im = gp[buf, sl_re], gp[buf, sl_im], gq[buf, sl_re], gq[buf, sl_im]
            t_re = c_re * q_re + c_im * q_im
            t_im = c_im * q_re - c_re * q_im
            sum_re += p_re * t_re - p_im * t_im
            sum_im += p_re * t_im + p_im * t_re
            put(2, kt, 0, t_re * t_re + t_im * t_im)
            put(2, kt, 1, (c_re * c_re + c_im * c_im) * (p_re * p_re + p_im * p_im))
        v_re, v_im = load_v(rsl)
        e_re = v_re - jnp.sum(sum_re, axis=0, keepdims=True)
        e_im = v_im - jnp.sum(sum_im, axis=0, keepdims=True)
        for kt in range(full_k // TILE):
            c_re, c_im = load_c(kt, rsl)
            sl_re, sl_im = pl.ds(kt * TILE, TILE), pl.ds(full_k + kt * TILE, TILE)
            p_re, p_im, q_re, q_im = gp[buf, sl_re], gp[buf, sl_im], gq[buf, sl_re], gq[buf, sl_im]
            d_re = e_re * c_re + e_im * c_im
            d_im = e_im * c_re - e_re * c_im
            put(0, kt, 0, d_re * q_re - d_im * q_im)
            put(1, kt, 0, d_re * q_im + d_im * q_re)
            put(0, kt, 1, d_re * p_re + d_im * p_im)
            put(1, kt, 1, d_re * p_im - d_im * p_re)
        part = jnp.dot(xs[buf], tt[rc], preferred_element_type=jnp.float32)
        total = part if total is None else total + part

    def pack(kind):
        x = total[kind * full_k : (kind + 1) * full_k]
        return jnp.where(low, x[:half_k], x[half_k:])

    den = pack(2)
    return pack(0) + g_re * den, pack(1) + g_im * den, den


def sums_kernel(whole_tiles, g_ref, coh_ref, tail_ref, vis_ref, t1, t2, tt, out_ref, gp, gq, xs):
    rows = t1.shape[1]

    def load_c(kt, rsl):
        if kt < whole_tiles:
            return (coh_ref[0, 0, pl.ds(kt * TILE, TILE), rsl], coh_ref[1, 0, pl.ds(kt * TILE, TILE), rsl])
        sl = pl.ds((kt - whole_tiles) * TILE, TILE)
        return tail_ref[0, 0, sl, rsl], tail_ref[1, 0, sl, rsl]

    def load_v(rsl):
        return vis_ref[0, 0, :, rsl], vis_ref[1, 0, :, rsl]

    half_k = out_ref.shape[2]
    re, im, den = band_sums(g_ref[0, 0], g_ref[0, 1], load_c, load_v, rows, t1, t2, tt, gp, gq, xs)
    out_ref[0, 0] = re
    out_ref[0, 1] = im
    out_ref[0, 2] = den


def tables(station_first, station_second):
    def gather_table(station):
        return (lax.broadcasted_iota(jnp.int32, (LANES, 1), 0) % HALF == station[None, :]).astype(jnp.bfloat16)

    first = station_first.reshape(-1, 1, CHUNK)
    second = station_second.reshape(-1, 1, CHUNK)
    both = jnp.concatenate([first, first, second, second], axis=1).reshape(first.shape[0], 4 * CHUNK, 1)
    spread = (both == lax.broadcasted_iota(jnp.int32, (1, 1, LANES), 2) % HALF).astype(jnp.bfloat16)
    return gather_table(station_first), gather_table(station_second), spread


def packer(stations, bands, directions, half_k):
    def pack(x, fill=0.0):
        c = x.shape[0]
        x = x.reshape(c, x.shape[1], bands, directions)
        x = jnp.pad(x, ((0, 0), (0, HALF - x.shape[1]), (0, 0), (0, 2 * half_k - directions)), constant_values=fill)
        x = x.reshape(c, HALF, bands, 2, half_k).transpose(2, 0, 4, 3, 1)
        return x.reshape(bands, c, half_k, LANES)

    def unpack(x):
        c = x.shape[1]
        x = x.reshape(bands, c, half_k, 2, HALF).transpose(1, 4, 0, 3, 2)
        x = x.reshape(c, HALF, bands, 2 * half_k)[:, :stations, :, :directions]
        return x.reshape(c, stations, bands * directions)

    return pack, unpack


def on_device(visibility, coherency, station_first, station_second, gains_start, consensus_prev, dual_prev, penalty, noise_var):
    stations = gains_start.shape[1]
    directions = penalty.shape[0]
    bands = visibility.shape[1]
    rows = visibility.shape[2]
    groups = lax.axis_size("blk")
    bands_all = bands * lax.axis_size("band")
    full_k = round_up(directions, TILE)
    half_k = full_k // 2
    whole_tiles = directions // TILE
    t1, t2, tt = tables(station_first, station_second)
    tail = jnp.pad(coherency[:, :, whole_tiles * TILE :, :], ((0, 0), (0, 0), (0, full_k - directions), (0, 0)))
    tail = tail if full_k > whole_tiles * TILE else coherency[:, :, :TILE, :]
    pack, unpack = packer(stations, bands, directions, half_k)
    rho_col = jnp.tile(penalty, bands)
    scaled = dual_prev / rho_col
    target = pack(consensus_prev - scaled)
    rho_pack = jnp.pad(penalty, (0, full_k - directions), constant_values=1.0).reshape(2, half_k).T
    weight = jnp.repeat(rho_pack * (rows * groups / (stations * directions)), HALF, axis=1)
    gains = pack(gains_start)
    vis = visibility[:, :, None, :]
    whole = lambda f: (0, 0)
    call = pl.pallas_call(
        functools.partial(sums_kernel, whole_tiles),
        out_shape=jax.ShapeDtypeStruct((bands, 3, half_k, LANES), jnp.float32),
        grid=(bands,),
        in_specs=[
            pl.BlockSpec((1, 2, half_k, LANES), lambda f: (f, 0, 0, 0)),
            pl.BlockSpec((2, 1, directions, rows), lambda f: (0, f, 0, 0)),
            pl.BlockSpec((2, 1, tail.shape[2], rows), lambda f: (0, f, 0, 0)),
            pl.BlockSpec((2, 1, 1, rows), lambda f: (0, f, 0, 0)),
            pl.BlockSpec((LANES, rows), whole),
            pl.BlockSpec((LANES, rows), whole),
            pl.BlockSpec((rows // CHUNK, 4 * CHUNK, LANES), lambda f: (0, 0, 0)),
        ],
        out_specs=pl.BlockSpec((1, 3, half_k, LANES), lambda f: (f, 0, 0, 0)),
        scratch_shapes=[
            pltpu.VMEM((2, 2 * full_k, CHUNK), jnp.float32),
            pltpu.VMEM((2, 2 * full_k, CHUNK), jnp.float32),
            pltpu.VMEM((2, 3 * full_k, 4 * CHUNK), jnp.bfloat16),
        ],
        compiler_params=pltpu.CompilerParams(vmem_limit_bytes=48 << 20),
        name="band_sums",
    )
    for step in range(ITERS):
        parts = call(gains, coherency, tail, vis, t1, t2, tt)
        total = lax.psum(parts, "blk")
        fresh = (total[:, :2] + weight * target) / (total[:, 2:] + weight)
        gains = 0.5 * gains + 0.5 * fresh
    gains = unpack(gains)
    mixed = gains + scaled
    smooth = smoother(noise_var, bands_all)[:, :, :directions]
    offset = lax.axis_index("band") * bands
    cols = lax.dynamic_slice_in_dim(smooth, offset, bands, 0)
    local_view = mixed.reshape(2, stations, bands, directions)
    term = jnp.einsum("gfk,cpgk->cpfk", cols, local_view, precision=lax.Precision.HIGHEST)
    term = term.reshape(2, stations, bands_all * directions)
    consensus = lax.psum_scatter(term, "band", scatter_dimension=2, tiled=True)
    dual = dual_prev + rho_col * (gains - consensus)
    return (gains, consensus, dual)


def solution(mesh):
    return jax.shard_map(
        on_device,
        mesh=mesh,
        in_specs=(
            P(None, "band", "blk"),
            P(None, "band", None, "blk"),
            P("blk"),
            P("blk"),
            P(None, None, "band"),
            P(None, None, "band"),
            P(None, None, "band"),
            P(),
            P(),
        ),
        out_specs=(P(None, None, "band"), P(None, None, "band"), P(None, None, "band")),
        check_vma=False,
    )
```

```python
import functools
import jax
import jax.numpy as jnp
from jax import lax
from jax.experimental import pallas as pl
from jax.experimental.pallas import tpu as pltpu
from jax.sharding import PartitionSpec as P

ITERS = 4
LANES = 128
HALF = 64
CHUNK = 256
TILE = 16


def round_up(x, m):
    return (x + m - 1) // m * m


def smoother_kernel(count, noise_ref, out_ref, work):
    level = noise_ref[...]
    cols = lax.broadcasted_iota(jnp.int32, (count, LANES), 0)
    for i in range(count):
        diff = (cols - i).astype(jnp.float32) / (count / 4.0)
        kern = jnp.exp(-0.5 * diff * diff)
        work[i, :count, :] = kern + jnp.where(cols == i, level, 0.0)
        work[i, count:, :] = kern

    def eliminate(p, carry):
        pivot = work[p, pl.ds(p, 1), :]
        row = work[p] / pivot
        for i in range(count):
            work[i] = work[i] - work[i, pl.ds(p, 1), :] * row
        work[p] = row
        return carry

    lax.fori_loop(0, count, eliminate, 0)
    for i in range(count):
        out_ref[i] = work[i, count:, :]


def smoother(noise, count):
    pad = jnp.pad(noise, (0, LANES * ((noise.shape[0] + LANES - 1) // LANES) - noise.shape[0]), constant_values=1.0)
    groups = pad.shape[0] // LANES
    return pl.pallas_call(
        functools.partial(smoother_kernel, count),
        out_shape=jax.ShapeDtypeStruct((count, count, groups * LANES), jnp.float32),
        grid=(groups,),
        in_specs=[pl.BlockSpec((1, LANES), lambda g: (0, g))],
        out_specs=pl.BlockSpec((count, count, LANES), lambda g: (0, 0, g)),
        scratch_shapes=[pltpu.VMEM((count, 2 * count, LANES), jnp.float32)],
        compiler_params=pltpu.CompilerParams(vmem_limit_bytes=16 << 20),
        name="smoother",
    )(pad[None, :])


def band_sums(g_re, g_im, load_c, load_v, rows, t1, t2, tt, gp, gq, xs):
    half_k = g_re.shape[0]
    full_k = 2 * half_k
    lane = lax.broadcasted_iota(jnp.int32, (half_k, LANES), 1)
    low = lane < HALF
    parts = []
    for g in (g_re, g_im):
        r = pltpu.roll(g, HALF, 1)
        for full in (jnp.where(low, g, r), jnp.where(low, r, g)):
            hi = full.astype(jnp.bfloat16).astype(jnp.float32)
            parts.append(jnp.where(low, hi, full - hi))
    lhs = jnp.concatenate(parts, axis=0).astype(jnp.bfloat16)
    total = None
    for rc in range(rows // CHUNK):
        buf = rc % 2
        rsl = pl.ds(rc * CHUNK, CHUNK)
        gp[buf] = jnp.dot(lhs, t1[:, rsl], preferred_element_type=jnp.float32)
        gq[buf] = jnp.dot(lhs, t2[:, rsl], preferred_element_type=jnp.float32)
        sum_re = jnp.zeros((TILE, CHUNK), jnp.float32)
        sum_im = jnp.zeros((TILE, CHUNK), jnp.float32)

        def put(kind, kt, side, x):
            hi = x.astype(jnp.bfloat16)
            lo = (x - hi.astype(jnp.float32)).astype(jnp.bfloat16)
            rsel = pl.ds(kind * full_k + kt * TILE, TILE)
            xs[buf, rsel, pl.ds(2 * side * CHUNK, CHUNK)] = hi
            xs[buf, rsel, pl.ds((2 * side + 1) * CHUNK, CHUNK)] = lo

        for kt in range(full_k // TILE):
            c_re, c_im = load_c(kt, rsl)
            sl_re, sl_im = pl.ds(kt * TILE, TILE), pl.ds(full_k + kt * TILE, TILE)
            p_re, p_im, q_re, q_im = gp[buf, sl_re], gp[buf, sl_im], gq[buf, sl_re], gq[buf, sl_im]
            t_re = c_re * q_re + c_im * q_im
            t_im = c_im * q_re - c_re * q_im
            sum_re += p_re * t_re - p_im * t_im
            sum_im += p_re * t_im + p_im * t_re
            put(2, kt, 0, t_re * t_re + t_im * t_im)
            put(2, kt, 1, (c_re * c_re + c_im * c_im) * (p_re * p_re + p_im * p_im))
        v_re, v_im = load_v(rsl)
        e_re = v_re - jnp.sum(sum_re, axis=0, keepdims=True)
        e_im = v_im - jnp.sum(sum_im, axis=0, keepdims=True)
        for kt in range(full_k // TILE):
            c_re, c_im = load_c(kt, rsl)
            sl_re, sl_im = pl.ds(kt * TILE, TILE), pl.ds(full_k + kt * TILE, TILE)
            p_re, p_im, q_re, q_im = gp[buf, sl_re], gp[buf, sl_im], gq[buf, sl_re], gq[buf, sl_im]
            d_re = e_re * c_re + e_im * c_im
            d_im = e_im * c_re - e_re * c_im
            put(0, kt, 0, d_re * q_re - d_im * q_im)
            put(1, kt, 0, d_re * q_im + d_im * q_re)
            put(0, kt, 1, d_re * p_re + d_im * p_im)
            put(1, kt, 1, d_re * p_im - d_im * p_re)
        part = jnp.dot(xs[buf], tt[rc], preferred_element_type=jnp.float32)
        total = part if total is None else total + part

    def pack(kind):
        x = total[kind * full_k : (kind + 1) * full_k]
        return jnp.where(low, x[:half_k], x[half_k:])

    den = pack(2)
    return pack(0) + g_re * den, pack(1) + g_im * den, den


MESH = pl.DeviceIdType.MESH
LAG_B, LAG_C, LAG_D = 2, 4, 6


def fused_kernel(
    whole_tiles, half_k, steps,
    g0, target, scaled, weight, smooth, coh_hbm, tail, vis, t1, t2, tt,
    gains_out, cons_out,
    coh, gfull, cfull, psend, yrecv, zbuf, zrecv, mix, mixrecv, gp, gq, xs,
    coh_sem, ysend_sem, yrecv_sem, zsend_sem, zrecv_sem, gz_send, gz_recv, gy_send, gy_recv,
    mix_send, mix_recv, cz_send, cz_recv, cy_send, cy_recv,
):
    bands, _, packed, _ = gfull.shape
    rows = t1.shape[1]
    nblk, nband = lax.axis_size("blk"), lax.axis_size("band")
    nz = nblk // 2
    piece = packed // nblk
    half = packed // 2
    me = lax.axis_index("blk")
    group = lax.axis_index("band")
    y, z = lax.rem(me, 2), me // 2
    partner = {"blk": z * 2 + (1 - y)}

    def peer(d):
        return {"blk": lax.rem(z + d, nz) * 2 + y}

    def band_peer(d):
        return {"band": lax.rem(group + d, nband)}

    def span(start, size):
        return pl.ds(pl.multiple_of(start, 8), size)

    def piece_of(zi):
        return span(y * half + zi * piece, piece)

    own = piece_of(z)
    own_half = span(y * half, half)
    other_half = span((1 - y) * half, half)

    def remote(src, dst, send, recv, device):
        return pltpu.make_async_remote_copy(
            src_ref=src, dst_ref=dst, send_sem=send, recv_sem=recv, device_id=device, device_id_type=MESH
        )

    def coh_copy(f):
        return pltpu.make_async_copy(coh_hbm.at[:, f], coh.at[f], coh_sem.at[f])

    def y_copy(f):
        return remote(psend.at[f, :, other_half], yrecv.at[f], ysend_sem.at[f], yrecv_sem.at[f], partner)

    def z_copy(f, d):
        where = span(lax.rem(z + d, nz) * piece, piece)
        return remote(zbuf.at[f, :, where], zrecv.at[f, d - 1], zsend_sem.at[f, d - 1], zrecv_sem.at[f, d - 1], peer(d))

    def all_z(buf, send, recv, f, d, incoming):
        where = piece_of(lax.rem(z + nz - d, nz)) if incoming else own
        return remote(buf.at[f, :, where], buf.at[f, :, where], send.at[f, d - 1], recv.at[f, d - 1], peer(d))

    def all_y(buf, send, recv, f, incoming):
        where = other_half if incoming else own_half
        return remote(buf.at[f, :, where], buf.at[f, :, where], send.at[f], recv.at[f], partner)

    def mix_copy(f, d):
        return remote(mix.at[f], mixrecv.at[d - 1, f], mix_send.at[f, d - 1], mix_recv.at[f, d - 1], band_peer(d))

    for f in range(bands):
        coh_copy(f).start()
    barrier = pltpu.get_barrier_semaphore()
    pl.semaphore_signal(barrier, inc=1, device_id=partner, device_id_type=MESH)
    for d in range(1, nz):
        pl.semaphore_signal(barrier, inc=1, device_id=peer(d), device_id_type=MESH)
    for d in range(1, nband):
        pl.semaphore_signal(barrier, inc=1, device_id=band_peer(d), device_id_type=MESH)
    gfull[...] = g0[...]
    psend[...] = jnp.zeros_like(psend)
    pl.semaphore_wait(barrier, nz + nband - 1)

    def compute(n):
        f = lax.rem(n, bands)

        @pl.when(n < bands)
        def _():
            coh_copy(f).wait()

        @pl.when(n >= bands)
        def _():
            all_y(gfull, gy_send, gy_recv, f, False).wait_send()
            all_y(gfull, gy_send, gy_recv, f, True).wait_recv()

        def load_c(kt, rsl):
            if kt < whole_tiles:
                return (coh[f, 0, pl.ds(kt * TILE, TILE), rsl], coh[f, 1, pl.ds(kt * TILE, TILE), rsl])
            sl = pl.ds((kt - whole_tiles) * TILE, TILE)
            return tail[0, f, sl, rsl], tail[1, f, sl, rsl]

        def load_v(rsl):
            return vis[0, pl.ds(f, 1), rsl], vis[1, pl.ds(f, 1), rsl]

        g_re, g_im = gfull[f, 0, :half_k], gfull[f, 1, :half_k]
        sums = band_sums(g_re, g_im, load_c, load_v, rows, t1, t2, tt, gp, gq, xs)
        for i in range(3):
            psend[f, i, :half_k] = sums[i]
        y_copy(f).start()

    def stage_b(n):
        f = lax.rem(n, bands)
        y_copy(f).wait()
        zbuf[f] = psend[f, :, own_half] + yrecv[f]
        for d in range(1, nz):
            z_copy(f, d).start()

    def stage_c(n):
        f = lax.rem(n, bands)
        total = zbuf[f, :, span(z * piece, piece)]
        for d in range(1, nz):
            z_copy(f, d).wait()
            total = total + zrecv[f, d - 1]
        w = weight[own]
        inverse = 0.5 / (total[2] + w)
        for c in range(2):
            fresh = (total[c] + w * target[f, c, own]) * inverse
            value = 0.5 * gfull[f, c, own] + fresh
            gfull[f, c, own] = value
            mix[f, c] = value + scaled[f, c, own]
        for d in range(1, nz):
            all_z(gfull, gz_send, gz_recv, f, d, False).start()

        @pl.when(n >= steps - bands)
        def _():
            for d in range(1, nband):
                mix_copy(f, d).start()

    def stage_d(n):
        f = lax.rem(n, bands)
        for d in range(1, nz):
            all_z(gfull, gz_send, gz_recv, f, d, False).wait_send()
            all_z(gfull, gz_send, gz_recv, f, d, True).wait_recv()
        all_y(gfull, gy_send, gy_recv, f, False).start()

    def turn(n, carry):
        @pl.when(n < steps)
        def _():
            compute(n)

        for lag, stage in ((LAG_B, stage_b), (LAG_C, stage_c), (LAG_D, stage_d)):
            @pl.when(jnp.logical_and(n >= lag, n < steps + lag))
            def _(lag=lag, stage=stage):
                stage(n - lag)

        return carry

    lax.fori_loop(0, steps + LAG_D, turn, 0)

    for d in range(1, nband):
        for f in range(bands):
            mix_copy(f, d).wait()

    def smooth_band(f, carry):
        acc = [jnp.zeros((piece, LANES), jnp.float32) for _ in range(2)]
        for d in range(nband):
            source = lax.rem(group + nband - d, nband)
            for h in range(bands):
                w = smooth[f, source * bands + h]
                for c in range(2):
                    acc[c] += w * (mix[h, c] if d == 0 else mixrecv[d - 1, h, c])
        for c in range(2):
            cfull[f, c, own] = acc[c]
        for d in range(1, nz):
            all_z(cfull, cz_send, cz_recv, f, d, False).start()
        return carry

    lax.fori_loop(0, bands, smooth_band, 0)

    def spread_y(f, carry):
        for d in range(1, nz):
            all_z(cfull, cz_send, cz_recv, f, d, False).wait_send()
            all_z(cfull, cz_send, cz_recv, f, d, True).wait_recv()
        all_y(cfull, cy_send, cy_recv, f, False).start()
        return carry

    lax.fori_loop(0, bands, spread_y, 0)

    def finish(f, carry):
        all_y(gfull, gy_send, gy_recv, f, False).wait_send()
        all_y(gfull, gy_send, gy_recv, f, True).wait_recv()
        gains_out[f] = gfull[f]
        all_y(cfull, cy_send, cy_recv, f, False).wait_send()
        all_y(cfull, cy_send, cy_recv, f, True).wait_recv()
        cons_out[f] = cfull[f]
        return carry

    lax.fori_loop(0, bands, finish, 0)


def tables(station_first, station_second):
    def gather_table(station):
        return (lax.broadcasted_iota(jnp.int32, (LANES, 1), 0) % HALF == station[None, :]).astype(jnp.bfloat16)

    first = station_first.reshape(-1, 1, CHUNK)
    second = station_second.reshape(-1, 1, CHUNK)
    both = jnp.concatenate([first, first, second, second], axis=1).reshape(first.shape[0], 4 * CHUNK, 1)
    spread = (both == lax.broadcasted_iota(jnp.int32, (1, 1, LANES), 2) % HALF).astype(jnp.bfloat16)
    return gather_table(station_first), gather_table(station_second), spread


def packer(stations, bands, directions, half_k, packed):
    def pack(x):
        c = x.shape[0]
        x = x.reshape(c, x.shape[1], bands, directions)
        x = jnp.pad(x, ((0, 0), (0, HALF - x.shape[1]), (0, 0), (0, 2 * half_k - directions)))
        x = x.reshape(c, HALF, bands, 2, half_k).transpose(2, 0, 4, 3, 1)
        x = x.reshape(bands, c, half_k, LANES)
        return jnp.pad(x, ((0, 0), (0, 0), (0, packed - half_k), (0, 0)))

    def unpack(x):
        c = x.shape[1]
        x = x[:, :, :half_k].reshape(bands, c, half_k, 2, HALF).transpose(1, 4, 0, 3, 2)
        x = x.reshape(c, HALF, bands, 2 * half_k)[:, :stations, :, :directions]
        return x.reshape(c, stations, bands * directions)

    return pack, unpack


def on_device(visibility, coherency, station_first, station_second, gains_start, consensus_prev, dual_prev, penalty, noise_var):
    stations = gains_start.shape[1]
    directions = penalty.shape[0]
    bands = visibility.shape[1]
    rows = visibility.shape[2]
    groups = lax.axis_size("blk")
    nband = lax.axis_size("band")
    bands_all = bands * nband
    full_k = round_up(directions, TILE)
    half_k = full_k // 2
    packed = round_up(half_k, 8 * groups)
    piece = packed // groups
    nz = groups // 2
    whole_tiles = directions // TILE
    t1, t2, tt = tables(station_first, station_second)
    tail = jnp.pad(coherency[:, :, whole_tiles * TILE :, :], ((0, 0), (0, 0), (0, full_k - directions), (0, 0)))
    tail = tail if full_k > whole_tiles * TILE else coherency[:, :, :TILE, :]
    pack, unpack = packer(stations, bands, directions, half_k, packed)
    rho_col = jnp.tile(penalty, bands)
    scaled = dual_prev / rho_col
    rho_pack = jnp.pad(penalty, (0, full_k - directions), constant_values=1.0).reshape(2, half_k).T
    rho_pack = jnp.pad(rho_pack, ((0, packed - half_k), (0, 0)), constant_values=1.0)
    weight = jnp.repeat(rho_pack * (rows * groups / (stations * directions)), HALF, axis=1)
    solved = smoother(noise_var, bands_all)[:, :, :full_k]
    solved = lax.dynamic_slice_in_dim(solved, lax.axis_index("band") * bands, bands, 1)
    solved = solved.reshape(bands_all, bands, 2, half_k)
    solved = jnp.pad(solved, ((0, 0), (0, 0), (0, 0), (0, packed - half_k)))
    me = lax.axis_index("blk")
    position = (me % 2) * (packed // 2) + (me // 2) * piece
    solved = lax.dynamic_slice_in_dim(solved, position, piece, 3).transpose(1, 0, 3, 2)
    smooth = jnp.repeat(solved, HALF, axis=3)
    vmem = pl.BlockSpec(memory_space=pltpu.VMEM)
    dma = pltpu.SemaphoreType.DMA
    full = jax.ShapeDtypeStruct((bands, 2, packed, LANES), jnp.float32)
    f32 = jnp.float32
    gains, consensus = pl.pallas_call(
        functools.partial(fused_kernel, whole_tiles, half_k, ITERS * bands),
        out_shape=(full, full),
        in_specs=[vmem] * 5 + [pl.BlockSpec(memory_space=pl.ANY)] + [vmem] * 5,
        out_specs=(vmem, vmem),
        scratch_shapes=[
            pltpu.VMEM((bands, 2, directions, rows), f32),
            pltpu.VMEM((bands, 2, packed, LANES), f32),
            pltpu.VMEM((bands, 2, packed, LANES), f32),
            pltpu.VMEM((bands, 3, packed, LANES), f32),
            pltpu.VMEM((bands, 3, packed // 2, LANES), f32),
            pltpu.VMEM((bands, 3, packed // 2, LANES), f32),
            pltpu.VMEM((bands, nz - 1, 3, piece, LANES), f32),
            pltpu.VMEM((bands, 2, piece, LANES), f32),
            pltpu.VMEM((nband - 1, bands, 2, piece, LANES), f32),
            pltpu.VMEM((2, 2 * full_k, CHUNK), f32),
            pltpu.VMEM((2, 2 * full_k, CHUNK), f32),
            pltpu.VMEM((2, 3 * full_k, 4 * CHUNK), jnp.bfloat16),
            dma((bands,)),
            dma((bands,)), dma((bands,)),
            dma((bands, nz - 1)), dma((bands, nz - 1)),
            dma((bands, nz - 1)), dma((bands, nz - 1)),
            dma((bands,)), dma((bands,)),
            dma((bands, nband - 1)), dma((bands, nband - 1)),
            dma((bands, nz - 1)), dma((bands, nz - 1)),
            dma((bands,)), dma((bands,)),
        ],
        compiler_params=pltpu.CompilerParams(collective_id=0, has_side_effects=True, vmem_limit_bytes=56 << 20),
        name="admm",
    )(pack(gains_start), pack(consensus_prev - scaled), pack(scaled), weight, smooth, coherency, tail, visibility, t1, t2, tt)
    gains = unpack(gains)
    consensus = unpack(consensus)
    dual = dual_prev + rho_col * (gains - consensus)
    return (gains, consensus, dual)


def solution(mesh):
    return jax.shard_map(
        on_device,
        mesh=mesh,
        in_specs=(
            P(None, "band", "blk"),
            P(None, "band", None, "blk"),
            P("blk"),
            P("blk"),
            P(None, None, "band"),
            P(None, None, "band"),
            P(None, None, "band"),
            P(),
            P(),
        ),
        out_specs=(P(None, None, "band"), P(None, None, "band"), P(None, None, "band")),
        check_vma=False,
    )
```

```python
import functools
import jax
import jax.numpy as jnp
from jax import lax
from jax.experimental import pallas as pl
from jax.experimental.pallas import tpu as pltpu
from jax.sharding import PartitionSpec as P

ITERS = 4
LANES = 128
HALF = 64
CHUNK = 256
TILE = 16


def round_up(x, m):
    return (x + m - 1) // m * m


def invert(count, level, work):
    lanes = level.shape[1]
    cols = lax.broadcasted_iota(jnp.int32, (count, lanes), 0)
    for i in range(count):
        diff = (cols - i).astype(jnp.float32) / (count / 4.0)
        work[i] = jnp.exp(-0.5 * diff * diff) + jnp.where(cols == i, level, 0.0)

    def eliminate(p, carry):
        inverse = 1.0 / work[p, pl.ds(p, 1), :]
        at = cols == p
        row = jnp.where(at, 1.0, work[p]) * inverse
        for i in range(count):
            factor = work[i, pl.ds(p, 1), :]
            work[i] = jnp.where(at, 0.0, work[i]) - factor * row
        work[p] = row
        return carry

    lax.fori_loop(0, count, eliminate, 0)


def arrange_smoother(level, work, smooth, first_band, position, half_k):
    bands, count, piece, _ = smooth.shape
    lanes = level.shape[1]
    cols = lax.broadcasted_iota(jnp.int32, (count, lanes), 0)
    mats = []
    for f in range(bands):
        eye = jnp.where(cols == first_band + f, 1.0, 0.0)
        mats.append(eye - level * work[first_band + f])
    mats = jnp.concatenate(mats, axis=0)
    hi = mats.astype(jnp.bfloat16)
    rest = mats - hi.astype(jnp.float32)
    mid = rest.astype(jnp.bfloat16)
    low = (rest - mid.astype(jnp.float32)).astype(jnp.bfloat16)
    direction = lax.broadcasted_iota(jnp.int32, (lanes, LANES), 0)
    lane = lax.broadcasted_iota(jnp.int32, (lanes, LANES), 1)
    for j in range(piece):
        wanted = jnp.where(lane < HALF, 0, half_k) + position + j
        pick = jnp.where(direction == wanted, 1.0, 0.0).astype(jnp.bfloat16)
        rows = sum(jnp.dot(x, pick, preferred_element_type=jnp.float32) for x in (hi, mid, low))
        for f in range(bands):
            smooth[f, :, j, :] = rows[f * count : (f + 1) * count]


def build_tables(first, second, t1, t2, tt):
    rows = t1.shape[1]
    slot = lax.rem(lax.broadcasted_iota(jnp.int32, (LANES, CHUNK), 0), HALF)
    for rc in range(rows // CHUNK):
        rsl = pl.ds(rc * CHUNK, CHUNK)
        for side, (stations, table) in enumerate(((first, t1), (second, t2))):
            hot = jnp.where(slot == stations[:, rsl], 1.0, 0.0)
            table[:, rsl] = hot.astype(jnp.bfloat16)
            turned = jnp.transpose(hot).astype(jnp.bfloat16)
            for part in range(2):
                tt[rc, pl.ds((2 * side + part) * CHUNK, CHUNK), :] = turned


def band_sums(g_re, g_im, load_c, load_v, rows, t1, t2, tt, gp, gq, xs):
    half_k = g_re.shape[0]
    full_k = 2 * half_k
    lane = lax.broadcasted_iota(jnp.int32, (half_k, LANES), 1)
    low = lane < HALF
    parts = []
    for g in (g_re, g_im):
        r = pltpu.roll(g, HALF, 1)
        for full in (jnp.where(low, g, r), jnp.where(low, r, g)):
            hi = full.astype(jnp.bfloat16).astype(jnp.float32)
            parts.append(jnp.where(low, hi, full - hi))
    lhs = jnp.concatenate(parts, axis=0).astype(jnp.bfloat16)
    total = None

    def gather(rc):
        rsl = pl.ds(rc * CHUNK, CHUNK)
        gp[rc % 2] = jnp.dot(lhs, t1[:, rsl], preferred_element_type=jnp.float32)
        gq[rc % 2] = jnp.dot(lhs, t2[:, rsl], preferred_element_type=jnp.float32)

    gather(0)
    for rc in range(rows // CHUNK):
        buf = rc % 2
        rsl = pl.ds(rc * CHUNK, CHUNK)
        if rc + 1 < rows // CHUNK:
            gather(rc + 1)
        sum_re = jnp.zeros((TILE, CHUNK), jnp.float32)
        sum_im = jnp.zeros((TILE, CHUNK), jnp.float32)

        def put(kind, kt, side, x):
            hi = x.astype(jnp.bfloat16)
            lo = (x - hi.astype(jnp.float32)).astype(jnp.bfloat16)
            rsel = pl.ds(kind * full_k + kt * TILE, TILE)
            xs[buf, rsel, pl.ds(2 * side * CHUNK, CHUNK)] = hi
            xs[buf, rsel, pl.ds((2 * side + 1) * CHUNK, CHUNK)] = lo

        for kt in range(full_k // TILE):
            c_re, c_im = load_c(kt, rsl)
            sl_re, sl_im = pl.ds(kt * TILE, TILE), pl.ds(full_k + kt * TILE, TILE)
            p_re, p_im, q_re, q_im = gp[buf, sl_re], gp[buf, sl_im], gq[buf, sl_re], gq[buf, sl_im]
            t_re = c_re * q_re + c_im * q_im
            t_im = c_im * q_re - c_re * q_im
            sum_re += p_re * t_re - p_im * t_im
            sum_im += p_re * t_im + p_im * t_re
            put(2, kt, 0, t_re * t_re + t_im * t_im)
            put(2, kt, 1, (c_re * c_re + c_im * c_im) * (p_re * p_re + p_im * p_im))
        v_re, v_im = load_v(rsl)
        e_re = v_re - jnp.sum(sum_re, axis=0, keepdims=True)
        e_im = v_im - jnp.sum(sum_im, axis=0, keepdims=True)
        for kt in range(full_k // TILE):
            c_re, c_im = load_c(kt, rsl)
            sl_re, sl_im = pl.ds(kt * TILE, TILE), pl.ds(full_k + kt * TILE, TILE)
            p_re, p_im, q_re, q_im = gp[buf, sl_re], gp[buf, sl_im], gq[buf, sl_re], gq[buf, sl_im]
            d_re = e_re * c_re + e_im * c_im
            d_im = e_im * c_re - e_re * c_im
            put(0, kt, 0, d_re * q_re - d_im * q_im)
            put(1, kt, 0, d_re * q_im + d_im * q_re)
            put(0, kt, 1, d_re * p_re + d_im * p_im)
            put(1, kt, 1, d_re * p_im - d_im * p_re)
        part = jnp.dot(xs[buf], tt[rc], preferred_element_type=jnp.float32)
        total = part if total is None else total + part

    def pack(kind):
        x = total[kind * full_k : (kind + 1) * full_k]
        return jnp.where(low, x[:half_k], x[half_k:])

    den = pack(2)
    return pack(0) + g_re * den, pack(1) + g_im * den, den


MESH = pl.DeviceIdType.MESH
LAG_B, LAG_C, LAG_D = 2, 4, 6


def fused_kernel(
    half_k, steps, weight_per_rho,
    state, rho, noise, coh_hbm, vis, first, second,
    out,
    t1, t2, tt, work, smooth, coh, tail, gfull, cfull, psend, yrecv, zbuf, zrecv, mix, mixrecv, gp, gq, xs,
    coh_sem, ysend_sem, yrecv_sem, zsend_sem, zrecv_sem, gz_send, gz_recv, gy_send, gy_recv,
    mix_send, mix_recv, cz_send, cz_recv, cy_send, cy_recv,
):
    bands, _, packed, _ = gfull.shape
    directions = coh_hbm.shape[1]
    whole = directions // TILE * TILE
    rows = t1.shape[1]
    nblk, nband = lax.axis_size("blk"), lax.axis_size("band")
    nz = nblk // 2
    piece = packed // nblk
    half = packed // 2
    me = lax.axis_index("blk")
    group = lax.axis_index("band")
    y, z = lax.rem(me, 2), me // 2
    partner = {"blk": z * 2 + (1 - y)}

    def peer(d):
        return {"blk": lax.rem(z + d, nz) * 2 + y}

    def band_peer(d):
        return {"band": lax.rem(group + d, nband)}

    def span(start, size):
        return pl.ds(pl.multiple_of(start, 8), size)

    def piece_of(zi):
        return span(y * half + zi * piece, piece)

    own = piece_of(z)
    own_half = span(y * half, half)
    other_half = span((1 - y) * half, half)

    def remote(src, dst, send, recv, device):
        return pltpu.make_async_remote_copy(
            src_ref=src, dst_ref=dst, send_sem=send, recv_sem=recv, device_id=device, device_id_type=MESH
        )

    def coh_copy(f):
        return pltpu.make_async_copy(coh_hbm.at[:, :, f], coh.at[f], coh_sem.at[f])

    def y_copy(f):
        return remote(psend.at[f, :, other_half], yrecv.at[f], ysend_sem.at[f], yrecv_sem.at[f], partner)

    def z_copy(f, d):
        where = span(lax.rem(z + d, nz) * piece, piece)
        return remote(zbuf.at[f, :, where], zrecv.at[f, d - 1], zsend_sem.at[f, d - 1], zrecv_sem.at[f, d - 1], peer(d))

    def all_z(buf, send, recv, f, d, incoming):
        where = piece_of(lax.rem(z + nz - d, nz)) if incoming else own
        return remote(buf.at[f, :, where], buf.at[f, :, where], send.at[f, d - 1], recv.at[f, d - 1], peer(d))

    def all_y(buf, send, recv, f, incoming):
        where = other_half if incoming else own_half
        return remote(buf.at[f, :, where], buf.at[f, :, where], send.at[f], recv.at[f], partner)

    def mix_copy(f, d):
        return remote(mix.at[f], mixrecv.at[d - 1, f], mix_send.at[f, d - 1], mix_recv.at[f, d - 1], band_peer(d))

    for f in range(bands):
        coh_copy(f).start()
    barrier = pltpu.get_barrier_semaphore()
    pl.semaphore_signal(barrier, inc=1, device_id=partner, device_id_type=MESH)
    for d in range(1, nz):
        pl.semaphore_signal(barrier, inc=1, device_id=peer(d), device_id_type=MESH)
    for d in range(1, nband):
        pl.semaphore_signal(barrier, inc=1, device_id=band_peer(d), device_id_type=MESH)
    gfull[...] = state[:, 0:2]
    psend[...] = jnp.zeros_like(psend)
    tail[...] = jnp.zeros_like(tail)
    build_tables(first, second, t1, t2, tt)
    pl.semaphore_wait(barrier, nz + nband - 1)

    def compute(n):
        f = lax.rem(n, bands)

        @pl.when(n < bands)
        def _():
            coh_copy(f).wait()
            if directions > whole:
                for c in range(2):
                    tail[f, c, : directions - whole] = coh[f, c, whole:]

        @pl.when(n >= bands)
        def _():
            all_y(gfull, gy_send, gy_recv, f, False).wait_send()
            all_y(gfull, gy_send, gy_recv, f, True).wait_recv()

        def load_c(kt, rsl):
            if kt * TILE < whole:
                sl = pl.ds(kt * TILE, TILE)
                return coh[f, 0, sl, rsl], coh[f, 1, sl, rsl]
            return tail[f, 0, :, rsl], tail[f, 1, :, rsl]

        def load_v(rsl):
            return vis[0, pl.ds(f, 1), rsl], vis[1, pl.ds(f, 1), rsl]

        g_re, g_im = gfull[f, 0, :half_k], gfull[f, 1, :half_k]
        sums = band_sums(g_re, g_im, load_c, load_v, rows, t1, t2, tt, gp, gq, xs)
        for i in range(3):
            psend[f, i, :half_k] = sums[i]
        y_copy(f).start()

    def stage_b(n):
        f = lax.rem(n, bands)
        y_copy(f).wait()
        zbuf[f] = psend[f, :, own_half] + yrecv[f]
        for d in range(1, nz):
            z_copy(f, d).start()

    def stage_c(n):
        f = lax.rem(n, bands)
        total = zbuf[f, :, span(z * piece, piece)]
        for d in range(1, nz):
            z_copy(f, d).wait()
            total = total + zrecv[f, d - 1]
        w = rho[own] * weight_per_rho
        inverse = 0.5 / (total[2] + w)
        for c in range(2):
            scaled = state[f, 4 + c, own] / rho[own]
            fresh = (total[c] + w * (state[f, 2 + c, own] - scaled)) * inverse
            value = 0.5 * gfull[f, c, own] + fresh
            gfull[f, c, own] = value
            mix[f, c] = value + scaled
        for d in range(1, nz):
            all_z(gfull, gz_send, gz_recv, f, d, False).start()

        @pl.when(n >= steps - bands)
        def _():
            for d in range(1, nband):
                mix_copy(f, d).start()

    def stage_d(n):
        f = lax.rem(n, bands)
        for d in range(1, nz):
            all_z(gfull, gz_send, gz_recv, f, d, False).wait_send()
            all_z(gfull, gz_send, gz_recv, f, d, True).wait_recv()
        all_y(gfull, gy_send, gy_recv, f, False).start()

    def turn(n, carry):
        @pl.when(n < steps)
        def _():
            compute(n)

        for lag, stage in ((LAG_B, stage_b), (LAG_C, stage_c), (LAG_D, stage_d)):
            @pl.when(jnp.logical_and(n >= lag, n < steps + lag))
            def _(lag=lag, stage=stage):
                stage(n - lag)

        @pl.when(n == steps + LAG_B - 1)
        def _():
            invert(smooth.shape[1], noise[...], work)

        return carry

    lax.fori_loop(0, steps + LAG_D, turn, 0)

    arrange_smoother(noise[...], work, smooth, group * bands, y * half + z * piece, half_k)
    for d in range(1, nband):
        for f in range(bands):
            mix_copy(f, d).wait()

    def smooth_band(f, carry):
        acc = [jnp.zeros((piece, LANES), jnp.float32) for _ in range(2)]
        for d in range(nband):
            source = lax.rem(group + nband - d, nband)
            for h in range(bands):
                w = smooth[f, source * bands + h]
                for c in range(2):
                    acc[c] += w * (mix[h, c] if d == 0 else mixrecv[d - 1, h, c])
        for c in range(2):
            cfull[f, c, own] = acc[c]
        for d in range(1, nz):
            all_z(cfull, cz_send, cz_recv, f, d, False).start()
        return carry

    lax.fori_loop(0, bands, smooth_band, 0)

    def spread_y(f, carry):
        for d in range(1, nz):
            all_z(cfull, cz_send, cz_recv, f, d, False).wait_send()
            all_z(cfull, cz_send, cz_recv, f, d, True).wait_recv()
        all_y(cfull, cy_send, cy_recv, f, False).start()
        return carry

    lax.fori_loop(0, bands, spread_y, 0)

    def finish(f, carry):
        all_y(gfull, gy_send, gy_recv, f, False).wait_send()
        all_y(gfull, gy_send, gy_recv, f, True).wait_recv()
        all_y(cfull, cy_send, cy_recv, f, False).wait_send()
        all_y(cfull, cy_send, cy_recv, f, True).wait_recv()
        for c in range(2):
            g, cons = gfull[f, c], cfull[f, c]
            out[f, c] = g
            out[f, 2 + c] = cons
            out[f, 4 + c] = state[f, 4 + c] + rho[...] * (g - cons)
        return carry

    lax.fori_loop(0, bands, finish, 0)


def packer(stations, bands, directions, half_k, packed):
    def pack(x):
        c = x.shape[0]
        x = x.reshape(c, x.shape[1], bands, directions)
        x = jnp.pad(x, ((0, 0), (0, HALF - x.shape[1]), (0, 0), (0, 2 * half_k - directions)))
        x = x.reshape(c, HALF, bands, 2, half_k).transpose(2, 0, 4, 3, 1)
        x = x.reshape(bands, c, half_k, LANES)
        return jnp.pad(x, ((0, 0), (0, 0), (0, packed - half_k), (0, 0)))

    def unpack(x):
        c = x.shape[1]
        x = x[:, :, :half_k].reshape(bands, c, half_k, 2, HALF).transpose(1, 4, 0, 3, 2)
        x = x.reshape(c, HALF, bands, 2 * half_k)[:, :stations, :, :directions]
        return x.reshape(c, stations, bands * directions)

    return pack, unpack


def on_device(visibility, coherency, station_first, station_second, gains_start, consensus_prev, dual_prev, penalty, noise_var):
    stations = gains_start.shape[1]
    directions = penalty.shape[0]
    bands = visibility.shape[1]
    rows = visibility.shape[2]
    groups = lax.axis_size("blk")
    nband = lax.axis_size("band")
    bands_all = bands * nband
    full_k = round_up(directions, TILE)
    half_k = full_k // 2
    packed = round_up(half_k, 8 * groups)
    piece = packed // groups
    nz = groups // 2
    pack, unpack = packer(stations, bands, directions, half_k, packed)
    rho = jnp.pad(penalty, (0, full_k - directions), constant_values=1.0).reshape(2, half_k).T
    rho = jnp.pad(rho, ((0, packed - half_k), (0, 0)), constant_values=1.0)
    rho = jnp.repeat(rho, HALF, axis=1)
    lanes = round_up(full_k, LANES)
    noise = jnp.pad(noise_var, (0, lanes - directions), constant_values=1.0)[None, :]
    state = pack(jnp.concatenate([gains_start, consensus_prev, dual_prev], axis=0))
    vmem = pl.BlockSpec(memory_space=pltpu.VMEM)
    dma = pltpu.SemaphoreType.DMA
    f32, bf16 = jnp.float32, jnp.bfloat16
    out = pl.pallas_call(
        functools.partial(fused_kernel, half_k, ITERS * bands, rows * groups / (stations * directions)),
        out_shape=jax.ShapeDtypeStruct((bands, 6, packed, LANES), f32),
        in_specs=[vmem] * 3 + [pl.BlockSpec(memory_space=pl.ANY)] + [vmem] * 3,
        out_specs=vmem,
        scratch_shapes=[
            pltpu.VMEM((LANES, rows), bf16),
            pltpu.VMEM((LANES, rows), bf16),
            pltpu.VMEM((rows // CHUNK, 4 * CHUNK, LANES), bf16),
            pltpu.VMEM((bands_all, bands_all, lanes), f32),
            pltpu.VMEM((bands, bands_all, piece, LANES), f32),
            pltpu.VMEM((bands, 2, directions, rows), f32),
            pltpu.VMEM((bands, 2, TILE, rows), f32),
            pltpu.VMEM((bands, 2, packed, LANES), f32),
            pltpu.VMEM((bands, 2, packed, LANES), f32),
            pltpu.VMEM((bands, 3, packed, LANES), f32),
            pltpu.VMEM((bands, 3, packed // 2, LANES), f32),
            pltpu.VMEM((bands, 3, packed // 2, LANES), f32),
            pltpu.VMEM((bands, nz - 1, 3, piece, LANES), f32),
            pltpu.VMEM((bands, 2, piece, LANES), f32),
            pltpu.VMEM((nband - 1, bands, 2, piece, LANES), f32),
            pltpu.VMEM((2, 2 * full_k, CHUNK), f32),
            pltpu.VMEM((2, 2 * full_k, CHUNK), f32),
            pltpu.VMEM((2, 3 * full_k, 4 * CHUNK), bf16),
            dma((bands,)),
            dma((bands,)), dma((bands,)),
            dma((bands, nz - 1)), dma((bands, nz - 1)),
            dma((bands, nz - 1)), dma((bands, nz - 1)),
            dma((bands,)), dma((bands,)),
            dma((bands, nband - 1)), dma((bands, nband - 1)),
            dma((bands, nz - 1)), dma((bands, nz - 1)),
            dma((bands,)), dma((bands,)),
        ],
        compiler_params=pltpu.CompilerParams(collective_id=0, has_side_effects=True, vmem_limit_bytes=56 << 20),
        name="admm",
    )(state, rho, noise, coherency.transpose(0, 2, 1, 3), visibility, station_first[None, :], station_second[None, :])
    out = unpack(out)
    return (out[0:2], out[2:4], out[4:6])


def solution(mesh):
    return jax.shard_map(
        on_device,
        mesh=mesh,
        in_specs=(
            P(None, "band", "blk"),
            P(None, "band", None, "blk"),
            P("blk"),
            P("blk"),
            P(None, None, "band"),
            P(None, None, "band"),
            P(None, None, "band"),
            P(),
            P(),
        ),
        out_specs=(P(None, None, "band"), P(None, None, "band"), P(None, None, "band")),
        check_vma=False,
    )
```

```python
import functools
import jax
import jax.numpy as jnp
from jax import lax
from jax.experimental import pallas as pl
from jax.experimental.pallas import tpu as pltpu
from jax.sharding import PartitionSpec as P

ITERS = 4
LANES = 128
CHUNK = 256
TILE = 16


def round_up(x, m):
    return (x + m - 1) // m * m


def invert(count, level, work):
    lanes = level.shape[1]
    cols = lax.broadcasted_iota(jnp.int32, (count, lanes), 0)
    for i in range(count):
        diff = (cols - i).astype(jnp.float32) / (count / 4.0)
        work[i] = jnp.exp(-0.5 * diff * diff) + jnp.where(cols == i, level, 0.0)

    def eliminate(p, carry):
        inverse = 1.0 / work[p, pl.ds(p, 1), :]
        at = cols == p
        row = jnp.where(at, 1.0, work[p]) * inverse
        for i in range(count):
            factor = work[i, pl.ds(p, 1), :]
            work[i] = jnp.where(at, 0.0, work[i]) - factor * row
        work[p] = row
        return carry

    lax.fori_loop(0, count, eliminate, 0)


def build_tables(first, second, t1, t2, ts):
    twice, rows = t1.shape
    count = twice // 2
    slot = lax.rem(lax.broadcasted_iota(jnp.int32, (twice, CHUNK), 0), count)
    for rc in range(rows // CHUNK):
        rsl = pl.ds(rc * CHUNK, CHUNK)
        for side, (stations, table) in enumerate(((first, t1), (second, t2))):
            hot = jnp.where(slot == stations[:, rsl], 1.0, 0.0).astype(jnp.bfloat16)
            table[:, rsl] = hot
            for part in range(2):
                ts[rc, :, pl.ds((2 * side + part) * CHUNK, CHUNK)] = hot[:count]


def band_sums(g_re, g_im, load_c, load_v, rows, full_k, t1, t2, ts, gp, gq, xs):
    parts = []
    for g in (g_re, g_im):
        hi = g.astype(jnp.bfloat16).astype(jnp.float32)
        parts.append(jnp.transpose(jnp.concatenate([hi, g - hi], axis=0))[:full_k])
    lhs = jnp.concatenate(parts, axis=0).astype(jnp.bfloat16)
    total = None

    def gather(rc):
        rsl = pl.ds(rc * CHUNK, CHUNK)
        gp[rc % 2] = jnp.dot(lhs, t1[:, rsl], preferred_element_type=jnp.float32)
        gq[rc % 2] = jnp.dot(lhs, t2[:, rsl], preferred_element_type=jnp.float32)

    gather(0)
    for rc in range(rows // CHUNK):
        buf = rc % 2
        rsl = pl.ds(rc * CHUNK, CHUNK)
        if rc + 1 < rows // CHUNK:
            gather(rc + 1)
        sum_re = jnp.zeros((TILE, CHUNK), jnp.float32)
        sum_im = jnp.zeros((TILE, CHUNK), jnp.float32)

        def put(kind, kt, side, x):
            hi = x.astype(jnp.bfloat16)
            lo = (x - hi.astype(jnp.float32)).astype(jnp.bfloat16)
            rsel = pl.ds(kind * LANES + kt * TILE, TILE)
            xs[buf, rsel, pl.ds(2 * side * CHUNK, CHUNK)] = hi
            xs[buf, rsel, pl.ds((2 * side + 1) * CHUNK, CHUNK)] = lo

        for kt in range(full_k // TILE):
            c_re, c_im = load_c(kt, rsl)
            sl_re, sl_im = pl.ds(kt * TILE, TILE), pl.ds(full_k + kt * TILE, TILE)
            p_re, p_im, q_re, q_im = gp[buf, sl_re], gp[buf, sl_im], gq[buf, sl_re], gq[buf, sl_im]
            t_re = c_re * q_re + c_im * q_im
            t_im = c_im * q_re - c_re * q_im
            sum_re += p_re * t_re - p_im * t_im
            sum_im += p_re * t_im + p_im * t_re
            put(2, kt, 0, t_re * t_re + t_im * t_im)
            put(2, kt, 1, (c_re * c_re + c_im * c_im) * (p_re * p_re + p_im * p_im))
        v_re, v_im = load_v(rsl)
        e_re = v_re - jnp.sum(sum_re, axis=0, keepdims=True)
        e_im = v_im - jnp.sum(sum_im, axis=0, keepdims=True)
        for kt in range(full_k // TILE):
            c_re, c_im = load_c(kt, rsl)
            sl_re, sl_im = pl.ds(kt * TILE, TILE), pl.ds(full_k + kt * TILE, TILE)
            p_re, p_im, q_re, q_im = gp[buf, sl_re], gp[buf, sl_im], gq[buf, sl_re], gq[buf, sl_im]
            d_re = e_re * c_re + e_im * c_im
            d_im = e_im * c_re - e_re * c_im
            put(0, kt, 0, d_re * q_re - d_im * q_im)
            put(1, kt, 0, d_re * q_im + d_im * q_re)
            put(0, kt, 1, d_re * p_re + d_im * p_im)
            put(1, kt, 1, d_re * p_im - d_im * p_re)
        part = lax.dot_general(ts[rc], xs[buf], (((1,), (1,)), ((), ())), preferred_element_type=jnp.float32)
        total = part if total is None else total + part

    num_re, num_im, den = (total[:, i * LANES : (i + 1) * LANES] for i in range(3))
    return num_re + g_re * den, num_im + g_im * den, den


MESH = pl.DeviceIdType.MESH
LAG_B, LAG_C, LAG_D = 2, 4, 6


def fused_kernel(
    steps, weight_per_rho,
    gains_start, consensus_prev, dual_prev, levels, coh_hbm, vis, first, second,
    gains_out, cons_out, dual_out,
    t1, t2, ts, work, state, coh, tail, gfull, cfull, psend, yrecv, zbuf, zrecv, mix, mixrecv, gp, gq, xs,
    coh_sem, ysend_sem, yrecv_sem, zsend_sem, zrecv_sem, gz_send, gz_recv, gy_send, gy_recv,
    mix_send, mix_recv, cz_send, cz_recv, cy_send, cy_recv,
):
    bands, _, packed, _ = gfull.shape
    directions = coh_hbm.shape[1]
    whole = directions // TILE * TILE
    full_k = round_up(directions, TILE)
    rows = t1.shape[1]
    nblk, nband = lax.axis_size("blk"), lax.axis_size("band")
    nz = nblk // 2
    piece = packed // nblk
    half = packed // 2
    me = lax.axis_index("blk")
    group = lax.axis_index("band")
    y, z = lax.rem(me, 2), me // 2
    partner = {"blk": z * 2 + (1 - y)}

    def peer(d):
        return {"blk": lax.rem(z + d, nz) * 2 + y}

    def band_peer(d):
        return {"band": lax.rem(group + d, nband)}

    def span(start, size):
        return pl.ds(pl.multiple_of(start, 8), size)

    def piece_of(zi):
        return span(y * half + zi * piece, piece)

    own = piece_of(z)
    own_half = span(y * half, half)
    other_half = span((1 - y) * half, half)

    def remote(src, dst, send, recv, device):
        return pltpu.make_async_remote_copy(
            src_ref=src, dst_ref=dst, send_sem=send, recv_sem=recv, device_id=device, device_id_type=MESH
        )

    def coh_copy(f):
        return pltpu.make_async_copy(coh_hbm.at[:, :, f], coh.at[f], coh_sem.at[f])

    def y_copy(f):
        return remote(psend.at[f, :, other_half], yrecv.at[f], ysend_sem.at[f], yrecv_sem.at[f], partner)

    def z_copy(f, d):
        where = span(lax.rem(z + d, nz) * piece, piece)
        return remote(zbuf.at[f, :, where], zrecv.at[f, d - 1], zsend_sem.at[f, d - 1], zrecv_sem.at[f, d - 1], peer(d))

    def all_z(buf, send, recv, f, d, incoming):
        where = piece_of(lax.rem(z + nz - d, nz)) if incoming else own
        return remote(buf.at[f, :, where], buf.at[f, :, where], send.at[f, d - 1], recv.at[f, d - 1], peer(d))

    def all_y(buf, send, recv, f, incoming):
        where = other_half if incoming else own_half
        return remote(buf.at[f, :, where], buf.at[f, :, where], send.at[f], recv.at[f], partner)

    def mix_copy(f, d):
        return remote(mix.at[f], mixrecv.at[d - 1, f], mix_send.at[f, d - 1], mix_recv.at[f, d - 1], band_peer(d))

    for f in range(bands):
        coh_copy(f).start()
    barrier = pltpu.get_barrier_semaphore()
    pl.semaphore_signal(barrier, inc=1, device_id=partner, device_id_type=MESH)
    for d in range(1, nz):
        pl.semaphore_signal(barrier, inc=1, device_id=peer(d), device_id_type=MESH)
    for d in range(1, nband):
        pl.semaphore_signal(barrier, inc=1, device_id=band_peer(d), device_id_type=MESH)
    stations = gains_start.shape[1]
    rho, noise = levels[0:1], levels[1:2]

    def window(ref, c, f):
        begin = f * directions
        at = min(begin, bands * directions - LANES)
        value = ref[c, :, at : at + LANES]
        return pltpu.roll(value, LANES - (begin - at), 1) if begin > at else value

    if packed > stations:
        gfull[:, :, stations:] = jnp.zeros((bands, 2, packed - stations, LANES), jnp.float32)
        state[:, :, stations:] = jnp.zeros((bands, 4, packed - stations, LANES), jnp.float32)
    for f in range(bands):
        for c in range(2):
            gfull[f, c, :stations] = window(gains_start, c, f)
            scaled = window(dual_prev, c, f) / rho
            state[f, c, :stations] = window(consensus_prev, c, f) - scaled
            state[f, 2 + c, :stations] = scaled
    xs[...] = jnp.zeros_like(xs)
    tail[...] = jnp.zeros_like(tail)
    build_tables(first, second, t1, t2, ts)
    pl.semaphore_wait(barrier, nz + nband - 1)

    def compute(n):
        f = lax.rem(n, bands)

        @pl.when(n < bands)
        def _():
            coh_copy(f).wait()
            if directions > whole:
                for c in range(2):
                    tail[f, c, : directions - whole] = coh[f, c, whole:]

        @pl.when(n >= bands)
        def _():
            all_y(gfull, gy_send, gy_recv, f, False).wait_send()
            all_y(gfull, gy_send, gy_recv, f, True).wait_recv()

        def load_c(kt, rsl):
            if kt * TILE < whole:
                sl = pl.ds(kt * TILE, TILE)
                return coh[f, 0, sl, rsl], coh[f, 1, sl, rsl]
            return tail[f, 0, :, rsl], tail[f, 1, :, rsl]

        def load_v(rsl):
            return vis[0, pl.ds(f, 1), rsl], vis[1, pl.ds(f, 1), rsl]

        sums = band_sums(gfull[f, 0], gfull[f, 1], load_c, load_v, rows, full_k, t1, t2, ts, gp, gq, xs)
        for i in range(3):
            psend[f, i] = sums[i]
        y_copy(f).start()

    def stage_b(n):
        f = lax.rem(n, bands)
        y_copy(f).wait()
        zbuf[f] = psend[f, :, own_half] + yrecv[f]
        for d in range(1, nz):
            z_copy(f, d).start()

    def stage_c(n):
        f = lax.rem(n, bands)
        total = zbuf[f, :, span(z * piece, piece)]
        for d in range(1, nz):
            z_copy(f, d).wait()
            total = total + zrecv[f, d - 1]
        w = rho * weight_per_rho
        inverse = 0.5 / (total[2] + w)
        for c in range(2):
            fresh = (total[c] + w * state[f, c, own]) * inverse
            value = 0.5 * gfull[f, c, own] + fresh
            gfull[f, c, own] = value
            mix[f, c] = value + state[f, 2 + c, own]
        for d in range(1, nz):
            all_z(gfull, gz_send, gz_recv, f, d, False).start()

        @pl.when(n >= steps - bands)
        def _():
            for d in range(1, nband):
                mix_copy(f, d).start()

    def stage_d(n):
        f = lax.rem(n, bands)
        for d in range(1, nz):
            all_z(gfull, gz_send, gz_recv, f, d, False).wait_send()
            all_z(gfull, gz_send, gz_recv, f, d, True).wait_recv()
        all_y(gfull, gy_send, gy_recv, f, False).start()

    def turn(n, carry):
        @pl.when(n < steps)
        def _():
            compute(n)

        for lag, stage in ((LAG_B, stage_b), (LAG_C, stage_c), (LAG_D, stage_d)):
            @pl.when(jnp.logical_and(n >= lag, n < steps + lag))
            def _(lag=lag, stage=stage):
                stage(n - lag)

        @pl.when(n == steps + LAG_B - 1)
        def _():
            invert(work.shape[0], noise, work)

        return carry

    lax.fori_loop(0, steps + LAG_D, turn, 0)

    for d in range(1, nband):
        for f in range(bands):
            mix_copy(f, d).wait()

    def smooth_band(f, carry):
        acc = [jnp.zeros((piece, LANES), jnp.float32) for _ in range(2)]
        for d in range(nband):
            source = lax.rem(group + nband - d, nband)
            for h in range(bands):
                column = source * bands + h
                unit = jnp.where(column == group * bands + f, 1.0, 0.0)
                w = unit - noise * work[group * bands + f, pl.ds(column, 1), :]
                for c in range(2):
                    acc[c] += w * (mix[h, c] if d == 0 else mixrecv[d - 1, h, c])
        for c in range(2):
            cfull[f, c, own] = acc[c]
        for d in range(1, nz):
            all_z(cfull, cz_send, cz_recv, f, d, False).start()
        return carry

    lax.fori_loop(0, bands, smooth_band, 0)

    def spread_y(f, carry):
        for d in range(1, nz):
            all_z(cfull, cz_send, cz_recv, f, d, False).wait_send()
            all_z(cfull, cz_send, cz_recv, f, d, True).wait_recv()
        all_y(cfull, cy_send, cy_recv, f, False).start()
        return carry

    lax.fori_loop(0, bands, spread_y, 0)

    for f in range(bands):
        all_y(gfull, gy_send, gy_recv, f, False).wait_send()
        all_y(gfull, gy_send, gy_recv, f, True).wait_recv()
        at = pl.ds(f * directions, directions)
        for c in range(2):
            gains_out[c, :, at] = gfull[f, c, :stations, :directions]
    for f in range(bands):
        all_y(cfull, cy_send, cy_recv, f, False).wait_send()
        all_y(cfull, cy_send, cy_recv, f, True).wait_recv()
        at = pl.ds(f * directions, directions)
        for c in range(2):
            cons = cfull[f, c, :stations]
            change = rho * (gfull[f, c, :stations] - cons)
            cons_out[c, :, at] = cons[:, :directions]
            dual_out[c, :, at] = dual_prev[c, :, at] + change[:, :directions]


def on_device(visibility, coherency, station_first, station_second, gains_start, consensus_prev, dual_prev, penalty, noise_var):
    stations = gains_start.shape[1]
    directions = penalty.shape[0]
    bands = visibility.shape[1]
    rows = visibility.shape[2]
    groups = lax.axis_size("blk")
    nband = lax.axis_size("band")
    bands_all = bands * nband
    full_k = round_up(directions, TILE)
    packed = round_up(stations, 8 * groups)
    piece = packed // groups
    nz = groups // 2
    levels = jnp.pad(jnp.stack([penalty, noise_var]), ((0, 0), (0, LANES - directions)), constant_values=1.0)
    vmem = pl.BlockSpec(memory_space=pltpu.VMEM)
    dma = pltpu.SemaphoreType.DMA
    f32, bf16 = jnp.float32, jnp.bfloat16
    out = pl.pallas_call(
        functools.partial(fused_kernel, ITERS * bands, rows * groups / (stations * directions)),
        out_shape=(jax.ShapeDtypeStruct(gains_start.shape, f32),) * 3,
        in_specs=[vmem] * 4 + [pl.BlockSpec(memory_space=pl.ANY)] + [vmem] * 3,
        out_specs=(vmem, vmem, vmem),
        scratch_shapes=[
            pltpu.VMEM((2 * packed, rows), bf16),
            pltpu.VMEM((2 * packed, rows), bf16),
            pltpu.VMEM((rows // CHUNK, packed, 4 * CHUNK), bf16),
            pltpu.VMEM((bands_all, bands_all, LANES), f32),
            pltpu.VMEM((bands, 4, packed, LANES), f32),
            pltpu.VMEM((bands, 2, directions, rows), f32),
            pltpu.VMEM((bands, 2, TILE, rows), f32),
            pltpu.VMEM((bands, 2, packed, LANES), f32),
            pltpu.VMEM((bands, 2, packed, LANES), f32),
            pltpu.VMEM((bands, 3, packed, LANES), f32),
            pltpu.VMEM((bands, 3, packed // 2, LANES), f32),
            pltpu.VMEM((bands, 3, packed // 2, LANES), f32),
            pltpu.VMEM((bands, nz - 1, 3, piece, LANES), f32),
            pltpu.VMEM((bands, 2, piece, LANES), f32),
            pltpu.VMEM((nband - 1, bands, 2, piece, LANES), f32),
            pltpu.VMEM((2, 2 * full_k, CHUNK), f32),
            pltpu.VMEM((2, 2 * full_k, CHUNK), f32),
            pltpu.VMEM((2, 3 * LANES, 4 * CHUNK), bf16),
            dma((bands,)),
            dma((bands,)), dma((bands,)),
            dma((bands, nz - 1)), dma((bands, nz - 1)),
            dma((bands, nz - 1)), dma((bands, nz - 1)),
            dma((bands,)), dma((bands,)),
            dma((bands, nband - 1)), dma((bands, nband - 1)),
            dma((bands, nz - 1)), dma((bands, nz - 1)),
            dma((bands,)), dma((bands,)),
        ],
        compiler_params=pltpu.CompilerParams(collective_id=0, has_side_effects=True, vmem_limit_bytes=56 << 20),
        name="admm",
    )(gains_start, consensus_prev, dual_prev, levels, coherency.transpose(0, 2, 1, 3), visibility, station_first[None, :], station_second[None, :])
    return out


def solution(mesh):
    return jax.shard_map(
        on_device,
        mesh=mesh,
        in_specs=(
            P(None, "band", "blk"),
            P(None, "band", None, "blk"),
            P("blk"),
            P("blk"),
            P(None, None, "band"),
            P(None, None, "band"),
            P(None, None, "band"),
            P(),
            P(),
        ),
        out_specs=(P(None, None, "band"), P(None, None, "band"), P(None, None, "band")),
        check_vma=False,
    )
```

```python
import functools
import jax
import jax.numpy as jnp
from jax import lax
from jax.experimental import pallas as pl
from jax.experimental.pallas import tpu as pltpu
from jax.sharding import PartitionSpec as P

ITERS = 4
LANES = 128
CHUNK = 256
TILE = 16


def round_up(x, m):
    return (x + m - 1) // m * m


def invert(count, level, work):
    lanes = level.shape[1]
    cols = lax.broadcasted_iota(jnp.int32, (count, lanes), 0)
    for i in range(count):
        diff = (cols - i).astype(jnp.float32) / (count / 4.0)
        work[i] = jnp.exp(-0.5 * diff * diff) + jnp.where(cols == i, level, 0.0)

    def eliminate(p, carry):
        inverse = 1.0 / work[p, pl.ds(p, 1), :]
        at = cols == p
        row = jnp.where(at, 1.0, work[p]) * inverse
        for i in range(count):
            factor = work[i, pl.ds(p, 1), :]
            work[i] = jnp.where(at, 0.0, work[i]) - factor * row
        work[p] = row
        return carry

    lax.fori_loop(0, count, eliminate, 0)


def build_tables(first, second, t1, t2, ts):
    twice, rows = t1.shape
    count = twice // 2
    slot = lax.rem(lax.broadcasted_iota(jnp.int32, (twice, CHUNK), 0), count)
    for rc in range(rows // CHUNK):
        rsl = pl.ds(rc * CHUNK, CHUNK)
        for side, (stations, table) in enumerate(((first, t1), (second, t2))):
            hot = jnp.where(slot == stations[:, rsl], 1.0, 0.0).astype(jnp.bfloat16)
            table[:, rsl] = hot
            for part in range(2):
                ts[rc, :, pl.ds((2 * side + part) * CHUNK, CHUNK)] = hot[:count]


def band_sums(g_re, g_im, load_c, load_v, rows, full_k, t1, t2, ts, gp, gq, xs):
    parts = []
    for g in (g_re, g_im):
        hi = g.astype(jnp.bfloat16).astype(jnp.float32)
        parts.append(jnp.transpose(jnp.concatenate([hi, g - hi], axis=0))[:full_k])
    lhs = jnp.concatenate(parts, axis=0).astype(jnp.bfloat16)
    total = None

    def gather(rc):
        rsl = pl.ds(rc * CHUNK, CHUNK)
        gp[rc % 2] = jnp.dot(lhs, t1[:, rsl], preferred_element_type=jnp.float32)
        gq[rc % 2] = jnp.dot(lhs, t2[:, rsl], preferred_element_type=jnp.float32)

    gather(0)
    for rc in range(rows // CHUNK):
        buf = rc % 2
        rsl = pl.ds(rc * CHUNK, CHUNK)
        if rc + 1 < rows // CHUNK:
            gather(rc + 1)
        sum_re = jnp.zeros((TILE, CHUNK), jnp.float32)
        sum_im = jnp.zeros((TILE, CHUNK), jnp.float32)

        def put(kind, kt, side, x):
            hi = x.astype(jnp.bfloat16)
            lo = (x - hi.astype(jnp.float32)).astype(jnp.bfloat16)
            rsel = pl.ds(kind * LANES + kt * TILE, TILE)
            xs[buf, rsel, pl.ds(2 * side * CHUNK, CHUNK)] = hi
            xs[buf, rsel, pl.ds((2 * side + 1) * CHUNK, CHUNK)] = lo

        for kt in range(full_k // TILE):
            c_re, c_im = load_c(kt, rsl)
            sl_re, sl_im = pl.ds(kt * TILE, TILE), pl.ds(full_k + kt * TILE, TILE)
            p_re, p_im, q_re, q_im = gp[buf, sl_re], gp[buf, sl_im], gq[buf, sl_re], gq[buf, sl_im]
            t_re = c_re * q_re + c_im * q_im
            t_im = c_im * q_re - c_re * q_im
            sum_re += p_re * t_re - p_im * t_im
            sum_im += p_re * t_im + p_im * t_re
            put(2, kt, 0, t_re * t_re + t_im * t_im)
            put(2, kt, 1, (c_re * c_re + c_im * c_im) * (p_re * p_re + p_im * p_im))
        v_re, v_im = load_v(rsl)
        e_re = v_re - jnp.sum(sum_re, axis=0, keepdims=True)
        e_im = v_im - jnp.sum(sum_im, axis=0, keepdims=True)
        for kt in range(full_k // TILE):
            c_re, c_im = load_c(kt, rsl)
            sl_re, sl_im = pl.ds(kt * TILE, TILE), pl.ds(full_k + kt * TILE, TILE)
            p_re, p_im, q_re, q_im = gp[buf, sl_re], gp[buf, sl_im], gq[buf, sl_re], gq[buf, sl_im]
            d_re = e_re * c_re + e_im * c_im
            d_im = e_im * c_re - e_re * c_im
            put(0, kt, 0, d_re * q_re - d_im * q_im)
            put(1, kt, 0, d_re * q_im + d_im * q_re)
            put(0, kt, 1, d_re * p_re + d_im * p_im)
            put(1, kt, 1, d_re * p_im - d_im * p_re)
        part = lax.dot_general(ts[rc], xs[buf], (((1,), (1,)), ((), ())), preferred_element_type=jnp.float32)
        total = part if total is None else total + part

    num_re, num_im, den = (total[:, i * LANES : (i + 1) * LANES] for i in range(3))
    return num_re + g_re * den, num_im + g_im * den, den


MESH = pl.DeviceIdType.MESH
LAG_B, LAG_C, LAG_D = 2, 4, 6


def fused_kernel(
    steps, weight_per_rho,
    gains_hbm, cons_hbm, dual_hbm, levels, coh_hbm, vis, first, second,
    gains_to, cons_to, dual_to,
    gains_start, consensus_prev, dual_prev, gains_out, cons_out, dual_out, in_sem, out_sem,
    t1, t2, ts, work, state, coh, tail, gfull, cfull, psend, yrecv, zbuf, zrecv, mix, mixrecv, gp, gq, xs,
    coh_sem, ysend_sem, yrecv_sem, zsend_sem, zrecv_sem, gz_send, gz_recv, gy_send, gy_recv,
    mix_send, mix_recv, cz_send, cz_recv, cy_send, cy_recv,
):
    bands, _, packed, _ = gfull.shape
    directions = coh_hbm.shape[1]
    whole = directions // TILE * TILE
    full_k = round_up(directions, TILE)
    rows = t1.shape[1]
    nblk, nband = lax.axis_size("blk"), lax.axis_size("band")
    nz = nblk // 2
    piece = packed // nblk
    half = packed // 2
    me = lax.axis_index("blk")
    group = lax.axis_index("band")
    y, z = lax.rem(me, 2), me // 2
    partner = {"blk": z * 2 + (1 - y)}

    def peer(d):
        return {"blk": lax.rem(z + d, nz) * 2 + y}

    def band_peer(d):
        return {"band": lax.rem(group + d, nband)}

    def span(start, size):
        return pl.ds(pl.multiple_of(start, 8), size)

    def piece_of(zi):
        return span(y * half + zi * piece, piece)

    own = piece_of(z)
    own_half = span(y * half, half)
    other_half = span((1 - y) * half, half)

    def remote(src, dst, send, recv, device):
        return pltpu.make_async_remote_copy(
            src_ref=src, dst_ref=dst, send_sem=send, recv_sem=recv, device_id=device, device_id_type=MESH
        )

    def coh_copy(f):
        return pltpu.make_async_copy(coh_hbm.at[:, :, f], coh.at[f], coh_sem.at[f])

    def y_copy(f):
        return remote(psend.at[f, :, other_half], yrecv.at[f], ysend_sem.at[f], yrecv_sem.at[f], partner)

    def z_copy(f, d):
        where = span(lax.rem(z + d, nz) * piece, piece)
        return remote(zbuf.at[f, :, where], zrecv.at[f, d - 1], zsend_sem.at[f, d - 1], zrecv_sem.at[f, d - 1], peer(d))

    def all_z(buf, send, recv, f, d, incoming):
        where = piece_of(lax.rem(z + nz - d, nz)) if incoming else own
        return remote(buf.at[f, :, where], buf.at[f, :, where], send.at[f, d - 1], recv.at[f, d - 1], peer(d))

    def all_y(buf, send, recv, f, incoming):
        where = other_half if incoming else own_half
        return remote(buf.at[f, :, where], buf.at[f, :, where], send.at[f], recv.at[f], partner)

    def mix_copy(f, d):
        return remote(mix.at[f], mixrecv.at[d - 1, f], mix_send.at[f, d - 1], mix_recv.at[f, d - 1], band_peer(d))

    def load_copy(i, c):
        pair = ((gains_hbm, gains_start), (cons_hbm, consensus_prev), (dual_hbm, dual_prev))[i]
        return pltpu.make_async_copy(pair[0].at[:, c], pair[1].at[c], in_sem.at[i, c])

    def store_copy(i, c):
        pair = ((gains_out, gains_to), (cons_out, cons_to), (dual_out, dual_to))[i]
        return pltpu.make_async_copy(pair[0].at[c], pair[1].at[:, c], out_sem.at[i, c])

    halves = [(i, c) for i in range(3) for c in range(2)]
    for i, c in halves:
        load_copy(i, c).start()
    for f in range(bands):
        coh_copy(f).start()
    barrier = pltpu.get_barrier_semaphore()
    pl.semaphore_signal(barrier, inc=1, device_id=partner, device_id_type=MESH)
    for d in range(1, nz):
        pl.semaphore_signal(barrier, inc=1, device_id=peer(d), device_id_type=MESH)
    for d in range(1, nband):
        pl.semaphore_signal(barrier, inc=1, device_id=band_peer(d), device_id_type=MESH)
    stations = gains_start.shape[1]
    rho, noise = levels[0:1], levels[1:2]

    def window(ref, c, f):
        begin = f * directions
        at = min(begin, bands * directions - LANES)
        value = ref[c, :, at : at + LANES]
        return pltpu.roll(value, LANES - (begin - at), 1) if begin > at else value

    build_tables(first, second, t1, t2, ts)
    xs[...] = jnp.zeros_like(xs)
    tail[...] = jnp.zeros_like(tail)
    for i, c in halves:
        load_copy(i, c).wait()
    if packed > stations:
        gfull[:, :, stations:] = jnp.zeros((bands, 2, packed - stations, LANES), jnp.float32)
        state[:, :, stations:] = jnp.zeros((bands, 4, packed - stations, LANES), jnp.float32)
    for f in range(bands):
        for c in range(2):
            gfull[f, c, :stations] = window(gains_start, c, f)
            scaled = window(dual_prev, c, f) / rho
            state[f, c, :stations] = window(consensus_prev, c, f) - scaled
            state[f, 2 + c, :stations] = scaled
    pl.semaphore_wait(barrier, nz + nband - 1)

    def compute(n):
        f = lax.rem(n, bands)

        @pl.when(n < bands)
        def _():
            coh_copy(f).wait()
            if directions > whole:
                for c in range(2):
                    tail[f, c, : directions - whole] = coh[f, c, whole:]

        @pl.when(n >= bands)
        def _():
            all_y(gfull, gy_send, gy_recv, f, False).wait_send()
            all_y(gfull, gy_send, gy_recv, f, True).wait_recv()

        def load_c(kt, rsl):
            if kt * TILE < whole:
                sl = pl.ds(kt * TILE, TILE)
                return coh[f, 0, sl, rsl], coh[f, 1, sl, rsl]
            return tail[f, 0, :, rsl], tail[f, 1, :, rsl]

        def load_v(rsl):
            return vis[0, pl.ds(f, 1), rsl], vis[1, pl.ds(f, 1), rsl]

        sums = band_sums(gfull[f, 0], gfull[f, 1], load_c, load_v, rows, full_k, t1, t2, ts, gp, gq, xs)
        for i in range(3):
            psend[f, i] = sums[i]
        y_copy(f).start()

    def stage_b(n):
        f = lax.rem(n, bands)
        y_copy(f).wait()
        zbuf[f] = psend[f, :, own_half] + yrecv[f]
        for d in range(1, nz):
            z_copy(f, d).start()

    def stage_c(n):
        f = lax.rem(n, bands)
        total = zbuf[f, :, span(z * piece, piece)]
        for d in range(1, nz):
            z_copy(f, d).wait()
            total = total + zrecv[f, d - 1]
        w = rho * weight_per_rho
        inverse = 0.5 / (total[2] + w)
        for c in range(2):
            fresh = (total[c] + w * state[f, c, own]) * inverse
            value = 0.5 * gfull[f, c, own] + fresh
            gfull[f, c, own] = value
            mix[f, c] = value + state[f, 2 + c, own]
        for d in range(1, nz):
            all_z(gfull, gz_send, gz_recv, f, d, False).start()

        @pl.when(n >= steps - bands)
        def _():
            for d in range(1, nband):
                mix_copy(f, d).start()

    def stage_d(n):
        f = lax.rem(n, bands)
        for d in range(1, nz):
            all_z(gfull, gz_send, gz_recv, f, d, False).wait_send()
            all_z(gfull, gz_send, gz_recv, f, d, True).wait_recv()
        all_y(gfull, gy_send, gy_recv, f, False).start()

    def turn(n, carry):
        @pl.when(n < steps)
        def _():
            compute(n)

        for lag, stage in ((LAG_B, stage_b), (LAG_C, stage_c), (LAG_D, stage_d)):
            @pl.when(jnp.logical_and(n >= lag, n < steps + lag))
            def _(lag=lag, stage=stage):
                stage(n - lag)

        @pl.when(n == steps + LAG_B - 1)
        def _():
            invert(work.shape[0], noise, work)

        return carry

    lax.fori_loop(0, steps + LAG_D, turn, 0)

    for d in range(1, nband):
        for f in range(bands):
            mix_copy(f, d).wait()

    def smooth_band(f, carry):
        acc = [jnp.zeros((piece, LANES), jnp.float32) for _ in range(2)]
        for d in range(nband):
            source = lax.rem(group + nband - d, nband)
            for h in range(bands):
                column = source * bands + h
                unit = jnp.where(column == group * bands + f, 1.0, 0.0)
                w = unit - noise * work[group * bands + f, pl.ds(column, 1), :]
                for c in range(2):
                    acc[c] += w * (mix[h, c] if d == 0 else mixrecv[d - 1, h, c])
        for c in range(2):
            cfull[f, c, own] = acc[c]
        for d in range(1, nz):
            all_z(cfull, cz_send, cz_recv, f, d, False).start()
        return carry

    lax.fori_loop(0, bands, smooth_band, 0)

    def spread_y(f, carry):
        for d in range(1, nz):
            all_z(cfull, cz_send, cz_recv, f, d, False).wait_send()
            all_z(cfull, cz_send, cz_recv, f, d, True).wait_recv()
        all_y(cfull, cy_send, cy_recv, f, False).start()
        return carry

    lax.fori_loop(0, bands, spread_y, 0)

    for f in range(bands):
        all_y(gfull, gy_send, gy_recv, f, False).wait_send()
        all_y(gfull, gy_send, gy_recv, f, True).wait_recv()
        at = pl.ds(f * directions, directions)
        for c in range(2):
            gains_out[c, :, at] = gfull[f, c, :stations, :directions]
    for c in range(2):
        store_copy(0, c).start()
    for f in range(bands):
        all_y(cfull, cy_send, cy_recv, f, False).wait_send()
        all_y(cfull, cy_send, cy_recv, f, True).wait_recv()
        at = pl.ds(f * directions, directions)
        for c in range(2):
            cons = cfull[f, c, :stations]
            change = rho * (gfull[f, c, :stations] - cons)
            cons_out[c, :, at] = cons[:, :directions]
            dual_out[c, :, at] = dual_prev[c, :, at] + change[:, :directions]
    for c in range(2):
        store_copy(1, c).start()
        store_copy(2, c).start()
    for i, c in halves:
        store_copy(i, c).wait()


def on_device(visibility, coherency, station_first, station_second, gains_start, consensus_prev, dual_prev, penalty, noise_var):
    stations = gains_start.shape[1]
    directions = penalty.shape[0]
    bands = visibility.shape[1]
    rows = visibility.shape[2]
    groups = lax.axis_size("blk")
    nband = lax.axis_size("band")
    bands_all = bands * nband
    full_k = round_up(directions, TILE)
    packed = round_up(stations, 8 * groups)
    piece = packed // groups
    nz = groups // 2
    levels = jnp.pad(jnp.stack([penalty, noise_var]), ((0, 0), (0, LANES - directions)), constant_values=1.0)
    vmem = pl.BlockSpec(memory_space=pltpu.VMEM)
    anywhere = pl.BlockSpec(memory_space=pl.ANY)
    dma = pltpu.SemaphoreType.DMA
    f32, bf16 = jnp.float32, jnp.bfloat16
    out = pl.pallas_call(
        functools.partial(fused_kernel, ITERS * bands, rows * groups / (stations * directions)),
        out_shape=(jax.ShapeDtypeStruct((stations, 2, bands * directions), f32),) * 3,
        in_specs=[anywhere] * 3 + [vmem, anywhere] + [vmem] * 3,
        out_specs=(anywhere,) * 3,
        scratch_shapes=[
            *[pltpu.VMEM((2, stations, bands * directions), f32)] * 6,
            dma((3, 2)), dma((3, 2)),
            pltpu.VMEM((2 * packed, rows), bf16),
            pltpu.VMEM((2 * packed, rows), bf16),
            pltpu.VMEM((rows // CHUNK, packed, 4 * CHUNK), bf16),
            pltpu.VMEM((bands_all, bands_all, LANES), f32),
            pltpu.VMEM((bands, 4, packed, LANES), f32),
            pltpu.VMEM((bands, 2, directions, rows), f32),
            pltpu.VMEM((bands, 2, TILE, rows), f32),
            pltpu.VMEM((bands, 2, packed, LANES), f32),
            pltpu.VMEM((bands, 2, packed, LANES), f32),
            pltpu.VMEM((bands, 3, packed, LANES), f32),
            pltpu.VMEM((bands, 3, packed // 2, LANES), f32),
            pltpu.VMEM((bands, 3, packed // 2, LANES), f32),
            pltpu.VMEM((bands, nz - 1, 3, piece, LANES), f32),
            pltpu.VMEM((bands, 2, piece, LANES), f32),
            pltpu.VMEM((nband - 1, bands, 2, piece, LANES), f32),
            pltpu.VMEM((2, 2 * full_k, CHUNK), f32),
            pltpu.VMEM((2, 2 * full_k, CHUNK), f32),
            pltpu.VMEM((2, 3 * LANES, 4 * CHUNK), bf16),
            dma((bands,)),
            dma((bands,)), dma((bands,)),
            dma((bands, nz - 1)), dma((bands, nz - 1)),
            dma((bands, nz - 1)), dma((bands, nz - 1)),
            dma((bands,)), dma((bands,)),
            dma((bands, nband - 1)), dma((bands, nband - 1)),
            dma((bands, nz - 1)), dma((bands, nz - 1)),
            dma((bands,)), dma((bands,)),
        ],
        compiler_params=pltpu.CompilerParams(collective_id=0, has_side_effects=True, vmem_limit_bytes=56 << 20),
        name="admm",
    )(*(x.transpose(1, 0, 2) for x in (gains_start, consensus_prev, dual_prev)), levels, coherency.transpose(0, 2, 1, 3), visibility, station_first[None, :], station_second[None, :])
    return tuple(x.transpose(1, 0, 2) for x in out)


def solution(mesh):
    return jax.shard_map(
        on_device,
        mesh=mesh,
        in_specs=(
            P(None, "band", "blk"),
            P(None, "band", None, "blk"),
            P("blk"),
            P("blk"),
            P(None, None, "band"),
            P(None, None, "band"),
            P(None, None, "band"),
            P(),
            P(),
        ),
        out_specs=(P(None, None, "band"), P(None, None, "band"), P(None, None, "band")),
        check_vma=False,
    )
```

```python
import functools
import jax
import jax.numpy as jnp
from jax import lax
from jax.experimental import pallas as pl
from jax.experimental.pallas import tpu as pltpu
from jax.sharding import PartitionSpec as P

ITERS = 4
LANES = 128
CHUNK = 256
TILE = 16


def round_up(x, m):
    return (x + m - 1) // m * m


def invert(count, level, work):
    lanes = level.shape[1]
    cols = lax.broadcasted_iota(jnp.int32, (count, lanes), 0)
    for i in range(count):
        diff = (cols - i).astype(jnp.float32) / (count / 4.0)
        work[i] = jnp.exp(-0.5 * diff * diff) + jnp.where(cols == i, level, 0.0)

    def eliminate(p, carry):
        inverse = 1.0 / work[p, pl.ds(p, 1), :]
        at = cols == p
        row = jnp.where(at, 1.0, work[p]) * inverse
        for i in range(count):
            factor = work[i, pl.ds(p, 1), :]
            work[i] = jnp.where(at, 0.0, work[i]) - factor * row
        work[p] = row
        return carry

    lax.fori_loop(0, count, eliminate, 0)


def build_tables(first, second, t1, t2, ts):
    twice, rows = t1.shape
    count = twice // 2
    slot = lax.rem(lax.broadcasted_iota(jnp.int32, (twice, CHUNK), 0), count)
    for rc in range(rows // CHUNK):
        rsl = pl.ds(rc * CHUNK, CHUNK)
        for side, (stations, table) in enumerate(((first, t1), (second, t2))):
            hot = jnp.where(slot == stations[:, rsl], 1.0, 0.0).astype(jnp.bfloat16)
            table[:, rsl] = hot
            for part in range(2):
                ts[rc, :, pl.ds((2 * side + part) * CHUNK, CHUNK)] = hot[:count]


def band_sums(g_re, g_im, load_c, load_v, rows, full_k, t1, t2, ts, gp, gq, xs):
    parts = []
    for g in (g_re, g_im):
        hi = g.astype(jnp.bfloat16).astype(jnp.float32)
        parts.append(jnp.transpose(jnp.concatenate([hi, g - hi], axis=0))[:full_k])
    lhs = jnp.concatenate(parts, axis=0).astype(jnp.bfloat16)
    total = None

    def gather(rc):
        rsl = pl.ds(rc * CHUNK, CHUNK)
        gp[rc % 2] = jnp.dot(lhs, t1[:, rsl], preferred_element_type=jnp.float32)
        gq[rc % 2] = jnp.dot(lhs, t2[:, rsl], preferred_element_type=jnp.float32)

    gather(0)
    for rc in range(rows // CHUNK):
        buf = rc % 2
        rsl = pl.ds(rc * CHUNK, CHUNK)
        if rc + 1 < rows // CHUNK:
            gather(rc + 1)
        sum_re = jnp.zeros((TILE, CHUNK), jnp.float32)
        sum_im = jnp.zeros((TILE, CHUNK), jnp.float32)

        def put(kind, kt, side, x):
            hi = x.astype(jnp.bfloat16)
            lo = (x - hi.astype(jnp.float32)).astype(jnp.bfloat16)
            rsel = pl.ds(kind * LANES + kt * TILE, TILE)
            xs[buf, rsel, pl.ds(2 * side * CHUNK, CHUNK)] = hi
            xs[buf, rsel, pl.ds((2 * side + 1) * CHUNK, CHUNK)] = lo

        for kt in range(full_k // TILE):
            c_re, c_im = load_c(kt, rsl)
            sl_re, sl_im = pl.ds(kt * TILE, TILE), pl.ds(full_k + kt * TILE, TILE)
            p_re, p_im, q_re, q_im = gp[buf, sl_re], gp[buf, sl_im], gq[buf, sl_re], gq[buf, sl_im]
            t_re = c_re * q_re + c_im * q_im
            t_im = c_im * q_re - c_re * q_im
            sum_re += p_re * t_re - p_im * t_im
            sum_im += p_re * t_im + p_im * t_re
            put(2, kt, 0, t_re * t_re + t_im * t_im)
            put(2, kt, 1, (c_re * c_re + c_im * c_im) * (p_re * p_re + p_im * p_im))
        v_re, v_im = load_v(rsl)
        e_re = v_re - jnp.sum(sum_re, axis=0, keepdims=True)
        e_im = v_im - jnp.sum(sum_im, axis=0, keepdims=True)
        for kt in range(full_k // TILE):
            c_re, c_im = load_c(kt, rsl)
            sl_re, sl_im = pl.ds(kt * TILE, TILE), pl.ds(full_k + kt * TILE, TILE)
            p_re, p_im, q_re, q_im = gp[buf, sl_re], gp[buf, sl_im], gq[buf, sl_re], gq[buf, sl_im]
            d_re = e_re * c_re + e_im * c_im
            d_im = e_im * c_re - e_re * c_im
            put(0, kt, 0, d_re * q_re - d_im * q_im)
            put(1, kt, 0, d_re * q_im + d_im * q_re)
            put(0, kt, 1, d_re * p_re + d_im * p_im)
            put(1, kt, 1, d_re * p_im - d_im * p_re)
        part = lax.dot_general(ts[rc], xs[buf], (((1,), (1,)), ((), ())), preferred_element_type=jnp.float32)
        total = part if total is None else total + part

    num_re, num_im, den = (total[:, i * LANES : (i + 1) * LANES] for i in range(3))
    return num_re + g_re * den, num_im + g_im * den, den


MESH = pl.DeviceIdType.MESH
LAG_B, LAG_C, LAG_D = 1, 3, 5


def fused_kernel(
    steps, weight_per_rho,
    gains_hbm, cons_hbm, dual_hbm, levels, coh_hbm, vis, first, second,
    gains_to, cons_to, dual_to,
    gains_start, consensus_prev, dual_prev, gains_out, cons_out, dual_out, in_sem, out_sem,
    t1, t2, ts, work, state, coh, tail, gfull, cfull, psend, yrecv, zbuf, zrecv, mix, mixrecv, gp, gq, xs,
    coh_sem, ysend_sem, yrecv_sem, zsend_sem, zrecv_sem, gz_send, gz_recv, gy_send, gy_recv,
    mix_send, mix_recv, cz_send, cz_recv, cy_send, cy_recv,
):
    bands, _, packed, _ = gfull.shape
    directions = coh_hbm.shape[1]
    whole = directions // TILE * TILE
    full_k = round_up(directions, TILE)
    rows = t1.shape[1]
    nblk, nband = lax.axis_size("blk"), lax.axis_size("band")
    nz = nblk // 2
    piece = packed // nblk
    half = packed // 2
    me = lax.axis_index("blk")
    group = lax.axis_index("band")
    y, z = lax.rem(me, 2), me // 2
    partner = {"blk": z * 2 + (1 - y)}

    def peer(d):
        return {"blk": lax.rem(z + d, nz) * 2 + y}

    def band_peer(d):
        return {"band": lax.rem(group + d, nband)}

    def span(start, size):
        return pl.ds(pl.multiple_of(start, 8), size)

    def piece_of(zi):
        return span(y * half + zi * piece, piece)

    own = piece_of(z)
    own_half = span(y * half, half)
    other_half = span((1 - y) * half, half)

    def remote(src, dst, send, recv, device):
        return pltpu.make_async_remote_copy(
            src_ref=src, dst_ref=dst, send_sem=send, recv_sem=recv, device_id=device, device_id_type=MESH
        )

    def coh_copy(f):
        return pltpu.make_async_copy(coh_hbm.at[:, :, f], coh.at[f], coh_sem.at[f])

    def y_copy(f):
        return remote(psend.at[f, :, other_half], yrecv.at[f], ysend_sem.at[f], yrecv_sem.at[f], partner)

    def z_copy(f, d):
        where = span(lax.rem(z + d, nz) * piece, piece)
        return remote(zbuf.at[f, :, where], zrecv.at[f, d - 1], zsend_sem.at[f, d - 1], zrecv_sem.at[f, d - 1], peer(d))

    def all_z(buf, send, recv, f, d, incoming):
        where = piece_of(lax.rem(z + nz - d, nz)) if incoming else own
        return remote(buf.at[f, :, where], buf.at[f, :, where], send.at[f, d - 1], recv.at[f, d - 1], peer(d))

    def all_y(buf, send, recv, f, incoming):
        where = other_half if incoming else own_half
        return remote(buf.at[f, :, where], buf.at[f, :, where], send.at[f], recv.at[f], partner)

    def mix_copy(f, d):
        return remote(mix.at[f], mixrecv.at[d - 1, f], mix_send.at[f, d - 1], mix_recv.at[f, d - 1], band_peer(d))

    def load_copy(i, c):
        pair = ((gains_hbm, gains_start), (cons_hbm, consensus_prev), (dual_hbm, dual_prev))[i]
        return pltpu.make_async_copy(pair[0].at[:, c], pair[1].at[c], in_sem.at[i, c])

    def store_copy(i, c):
        pair = ((gains_out, gains_to), (cons_out, cons_to), (dual_out, dual_to))[i]
        return pltpu.make_async_copy(pair[0].at[c], pair[1].at[:, c], out_sem.at[i, c])

    halves = [(i, c) for i in range(3) for c in range(2)]
    for i, c in halves:
        load_copy(i, c).start()
    for f in range(bands):
        coh_copy(f).start()
    barrier = pltpu.get_barrier_semaphore()
    pl.semaphore_signal(barrier, inc=1, device_id=partner, device_id_type=MESH)
    for d in range(1, nz):
        pl.semaphore_signal(barrier, inc=1, device_id=peer(d), device_id_type=MESH)
    for d in range(1, nband):
        pl.semaphore_signal(barrier, inc=1, device_id=band_peer(d), device_id_type=MESH)
    stations = gains_start.shape[1]
    rho, noise = levels[0:1], levels[1:2]

    def window(ref, c, f):
        begin = f * directions
        at = min(begin, bands * directions - LANES)
        value = ref[c, :, at : at + LANES]
        return pltpu.roll(value, LANES - (begin - at), 1) if begin > at else value

    build_tables(first, second, t1, t2, ts)
    xs[...] = jnp.zeros_like(xs)
    tail[...] = jnp.zeros_like(tail)
    for i, c in halves:
        load_copy(i, c).wait()
    if packed > stations:
        gfull[:, :, stations:] = jnp.zeros((bands, 2, packed - stations, LANES), jnp.float32)
        state[:, :, stations:] = jnp.zeros((bands, 4, packed - stations, LANES), jnp.float32)
    for f in range(bands):
        for c in range(2):
            gfull[f, c, :stations] = window(gains_start, c, f)
            scaled = window(dual_prev, c, f) / rho
            state[f, c, :stations] = window(consensus_prev, c, f) - scaled
            state[f, 2 + c, :stations] = scaled
    pl.semaphore_wait(barrier, nz + nband - 1)

    def compute(n):
        f = lax.rem(n, bands)

        @pl.when(n < bands)
        def _():
            coh_copy(f).wait()
            if directions > whole:
                for c in range(2):
                    tail[f, c, : directions - whole] = coh[f, c, whole:]

        @pl.when(n >= bands)
        def _():
            all_y(gfull, gy_send, gy_recv, f, False).wait_send()
            all_y(gfull, gy_send, gy_recv, f, True).wait_recv()

        def load_c(kt, rsl):
            if kt * TILE < whole:
                sl = pl.ds(kt * TILE, TILE)
                return coh[f, 0, sl, rsl], coh[f, 1, sl, rsl]
            return tail[f, 0, :, rsl], tail[f, 1, :, rsl]

        def load_v(rsl):
            return vis[0, pl.ds(f, 1), rsl], vis[1, pl.ds(f, 1), rsl]

        sums = band_sums(gfull[f, 0], gfull[f, 1], load_c, load_v, rows, full_k, t1, t2, ts, gp, gq, xs)
        for i in range(3):
            psend[f, i] = sums[i]
        y_copy(f).start()

    def stage_b(n):
        f = lax.rem(n, bands)
        y_copy(f).wait()
        zbuf[f] = psend[f, :, own_half] + yrecv[f]
        for d in range(1, nz):
            z_copy(f, d).start()

    def stage_c(n):
        f = lax.rem(n, bands)
        total = zbuf[f, :, span(z * piece, piece)]
        for d in range(1, nz):
            z_copy(f, d).wait()
            total = total + zrecv[f, d - 1]
        w = rho * weight_per_rho
        inverse = 0.5 / (total[2] + w)
        for c in range(2):
            fresh = (total[c] + w * state[f, c, own]) * inverse
            value = 0.5 * gfull[f, c, own] + fresh
            gfull[f, c, own] = value
            mix[f, c] = value + state[f, 2 + c, own]
        for d in range(1, nz):
            all_z(gfull, gz_send, gz_recv, f, d, False).start()

        @pl.when(n >= steps - bands)
        def _():
            for d in range(1, nband):
                mix_copy(f, d).start()

    def stage_d(n):
        f = lax.rem(n, bands)
        for d in range(1, nz):
            all_z(gfull, gz_send, gz_recv, f, d, False).wait_send()
            all_z(gfull, gz_send, gz_recv, f, d, True).wait_recv()
        all_y(gfull, gy_send, gy_recv, f, False).start()

    def turn(n, carry):
        @pl.when(n < steps)
        def _():
            compute(n)

        for lag, stage in ((LAG_B, stage_b), (LAG_C, stage_c), (LAG_D, stage_d)):
            @pl.when(jnp.logical_and(n >= lag, n < steps + lag))
            def _(lag=lag, stage=stage):
                stage(n - lag)

        @pl.when(n == steps + LAG_B - 1)
        def _():
            invert(work.shape[0], noise, work)

        return carry

    lax.fori_loop(0, steps + LAG_D, turn, 0)

    for d in range(1, nband):
        for f in range(bands):
            mix_copy(f, d).wait()

    def smooth_band(f, carry):
        acc = [jnp.zeros((piece, LANES), jnp.float32) for _ in range(2)]
        for d in range(nband):
            source = lax.rem(group + nband - d, nband)
            for h in range(bands):
                column = source * bands + h
                unit = jnp.where(column == group * bands + f, 1.0, 0.0)
                w = unit - noise * work[group * bands + f, pl.ds(column, 1), :]
                for c in range(2):
                    acc[c] += w * (mix[h, c] if d == 0 else mixrecv[d - 1, h, c])
        for c in range(2):
            cfull[f, c, own] = acc[c]
        for d in range(1, nz):
            all_z(cfull, cz_send, cz_recv, f, d, False).start()
        return carry

    lax.fori_loop(0, bands, smooth_band, 0)

    def spread_y(f, carry):
        for d in range(1, nz):
            all_z(cfull, cz_send, cz_recv, f, d, False).wait_send()
            all_z(cfull, cz_send, cz_recv, f, d, True).wait_recv()
        all_y(cfull, cy_send, cy_recv, f, False).start()
        return carry

    lax.fori_loop(0, bands, spread_y, 0)

    for f in range(bands):
        all_y(gfull, gy_send, gy_recv, f, False).wait_send()
        all_y(gfull, gy_send, gy_recv, f, True).wait_recv()
        at = pl.ds(f * directions, directions)
        for c in range(2):
            gains_out[c, :, at] = gfull[f, c, :stations, :directions]
    for c in range(2):
        store_copy(0, c).start()
    for f in range(bands):
        all_y(cfull, cy_send, cy_recv, f, False).wait_send()
        all_y(cfull, cy_send, cy_recv, f, True).wait_recv()
        at = pl.ds(f * directions, directions)
        for c in range(2):
            cons = cfull[f, c, :stations]
            change = rho * (gfull[f, c, :stations] - cons)
            cons_out[c, :, at] = cons[:, :directions]
            dual_out[c, :, at] = dual_prev[c, :, at] + change[:, :directions]
    for c in range(2):
        store_copy(1, c).start()
        store_copy(2, c).start()
    for i, c in halves:
        store_copy(i, c).wait()


def on_device(visibility, coherency, station_first, station_second, gains_start, consensus_prev, dual_prev, penalty, noise_var):
    stations = gains_start.shape[1]
    directions = penalty.shape[0]
    bands = visibility.shape[1]
    rows = visibility.shape[2]
    groups = lax.axis_size("blk")
    nband = lax.axis_size("band")
    bands_all = bands * nband
    full_k = round_up(directions, TILE)
    packed = round_up(stations, 8 * groups)
    piece = packed // groups
    nz = groups // 2
    levels = jnp.pad(jnp.stack([penalty, noise_var]), ((0, 0), (0, LANES - directions)), constant_values=1.0)
    vmem = pl.BlockSpec(memory_space=pltpu.VMEM)
    anywhere = pl.BlockSpec(memory_space=pl.ANY)
    dma = pltpu.SemaphoreType.DMA
    f32, bf16 = jnp.float32, jnp.bfloat16
    out = pl.pallas_call(
        functools.partial(fused_kernel, ITERS * bands, rows * groups / (stations * directions)),
        out_shape=(jax.ShapeDtypeStruct((stations, 2, bands * directions), f32),) * 3,
        in_specs=[anywhere] * 3 + [vmem, anywhere] + [vmem] * 3,
        out_specs=(anywhere,) * 3,
        scratch_shapes=[
            *[pltpu.VMEM((2, stations, bands * directions), f32)] * 6,
            dma((3, 2)), dma((3, 2)),
            pltpu.VMEM((2 * packed, rows), bf16),
            pltpu.VMEM((2 * packed, rows), bf16),
            pltpu.VMEM((rows // CHUNK, packed, 4 * CHUNK), bf16),
            pltpu.VMEM((bands_all, bands_all, LANES), f32),
            pltpu.VMEM((bands, 4, packed, LANES), f32),
            pltpu.VMEM((bands, 2, directions, rows), f32),
            pltpu.VMEM((bands, 2, TILE, rows), f32),
            pltpu.VMEM((bands, 2, packed, LANES), f32),
            pltpu.VMEM((bands, 2, packed, LANES), f32),
            pltpu.VMEM((bands, 3, packed, LANES), f32),
            pltpu.VMEM((bands, 3, packed // 2, LANES), f32),
            pltpu.VMEM((bands, 3, packed // 2, LANES), f32),
            pltpu.VMEM((bands, nz - 1, 3, piece, LANES), f32),
            pltpu.VMEM((bands, 2, piece, LANES), f32),
            pltpu.VMEM((nband - 1, bands, 2, piece, LANES), f32),
            pltpu.VMEM((2, 2 * full_k, CHUNK), f32),
            pltpu.VMEM((2, 2 * full_k, CHUNK), f32),
            pltpu.VMEM((2, 3 * LANES, 4 * CHUNK), bf16),
            dma((bands,)),
            dma((bands,)), dma((bands,)),
            dma((bands, nz - 1)), dma((bands, nz - 1)),
            dma((bands, nz - 1)), dma((bands, nz - 1)),
            dma((bands,)), dma((bands,)),
            dma((bands, nband - 1)), dma((bands, nband - 1)),
            dma((bands, nz - 1)), dma((bands, nz - 1)),
            dma((bands,)), dma((bands,)),
        ],
        compiler_params=pltpu.CompilerParams(collective_id=0, has_side_effects=True, vmem_limit_bytes=56 << 20),
        name="admm",
    )(*(x.transpose(1, 0, 2) for x in (gains_start, consensus_prev, dual_prev)), levels, coherency.transpose(0, 2, 1, 3), visibility, station_first[None, :], station_second[None, :])
    return tuple(x.transpose(1, 0, 2) for x in out)


def solution(mesh):
    return jax.shard_map(
        on_device,
        mesh=mesh,
        in_specs=(
            P(None, "band", "blk"),
            P(None, "band", None, "blk"),
            P("blk"),
            P("blk"),
            P(None, None, "band"),
            P(None, None, "band"),
            P(None, None, "band"),
            P(),
            P(),
        ),
        out_specs=(P(None, None, "band"), P(None, None, "band"), P(None, None, "band")),
        check_vma=False,
    )
```
